32 devices in a mesh: ens: 2 (over y), gx: 4 (over z), gy: 2 (over x), lev: 2 (over core).
Axes of the slice: x: 2, y: 2, z: 4, core: 2. Of those that a mesh axis runs over, the one named last changes fastest.
Arguments:
- innovations: bfloat16 [8, 4, 256, 1024], P('ens', 'lev', 'gx', 'gy'), parts along dimension 0, may hold values from -18 to 18
- restrict_offsets: int32 [4, 2], P('lev'), may hold values from 0 to 3
- prolong_offsets: int32 [4, 2], P('lev'), may hold values from 0 to 3
- east_courant: float32 [8, 64, 256], P(('ens', 'lev'), 'gx', 'gy'), parts along dimension 0, may hold values from 0.05 to 0.45
- north_courant: float32 [8, 64, 256], P(('ens', 'lev'), 'gx', 'gy'), parts along dimension 0, may hold values from 0.05 to 0.45
- obs_weight: float32 [8, 64, 256], P(('ens', 'lev'), 'gx', 'gy'), parts along dimension 0, may hold values from 0.5 to 4
Outputs:
- increment_fine: float32 [8, 256, 1024], P(('ens', 'lev'), 'gx', 'gy'), parts along dimension 0
- residual_inner: float32 [8, 64, 256], P(('ens', 'lev'), 'gx', 'gy'), parts along dimension 0
The draws below stay inside these ranges and needn't reach their ends.
There are 2 independent parts, one for each index of `ens`. The reference program is written for one: setup_inputs(seed, part) draws one part's arguments, and reference() takes and returns one part's arrays. A program takes and returns all parts, laid end to end along the dimension named above; an argument that names none is the same for every part. Nothing has to cross between parts.
All inputs are finite; a program needn't handle non-finite values.
Results may differ from the reference program's by a relative error of at most 0.0003.
Values may be sent and summed in bfloat16 or wider, within the bound.
A program may use at most 64 MiB of HBM per device.

```python
import math
import jax
import jax.numpy as jnp
from jax import lax

TS = 4
ITERS = 2
NXF = 256
NYF = 1024
L = 4
NXC = 64
NYC = 256


def place_ends(entries, stream_key, smallest, high):
    longest = entries.shape.index(max(entries.shape))
    spots = []
    for shift in (0, 1):
        where = [jax.random.randint(jax.random.fold_in(stream_key, axis), (), 0, length) for axis, length in enumerate(entries.shape)]
        where[longest] = (where[longest] + shift) % entries.shape[longest]
        spots.append(tuple(where))
    return entries.at[spots[0]].set(smallest).at[spots[1]].set(high)


def block_scale(own_key, shape, pieces, least, largest):
    gain = 1.0
    for dim, parts in pieces:
        steps = jax.random.uniform(jax.random.fold_in(jax.random.fold_in(own_key, 6), dim), (parts,), jnp.float32, least / len(pieces), largest / len(pieces))
        gain = gain * jnp.repeat(jnp.exp(steps), shape[dim] // parts).reshape((-1,) + (1,) * (len(shape) - 1 - dim))
    return gain


def scatter_about(stream_key, shape, spread, reach, cuts=(), kind=jnp.bfloat16):
    level = block_scale(stream_key, shape, cuts, -0.22, 0.18) if cuts else 1.0
    entries = jax.random.normal(stream_key, shape, jnp.float32) * spread * level
    return jnp.minimum(jnp.maximum(entries, -reach), reach).astype(kind)


def setup_inputs(seed: int = 0, part: int = 0) -> dict:
    key_of = jax.random.split(jax.random.key(seed), 7)
    part_splits = jax.random.split(jax.random.fold_in(key_of[6], part), 7)
    return {
        "innovations": scatter_about(part_splits[0], (TS, L, NXF, NYF), 3.0, 18.0, ((1, 2), (2, 4), (3, 2))),
        "restrict_offsets": place_ends(jax.random.randint(key_of[1], (L, 2), 0, 4), jax.random.fold_in(key_of[1], 1), 0, 3).astype(jnp.int32),
        "prolong_offsets": place_ends(jax.random.randint(key_of[2], (L, 2), 0, 4), jax.random.fold_in(key_of[2], 1), 0, 3).astype(jnp.int32),
        "east_courant": jnp.clip(0.05 + 0.39999999 * jax.random.uniform(part_splits[3], (L, NXC, NYC), jnp.float32) ** block_scale(part_splits[3], (L, NXC, NYC), ((0, 2), (1, 4), (2, 2)), -0.2, 0.2), 0.05, 0.45),
        "north_courant": jnp.clip(0.05 + 0.39999999 * jax.random.uniform(part_splits[4], (L, NXC, NYC), jnp.float32) ** block_scale(part_splits[4], (L, NXC, NYC), ((0, 2), (1, 4), (2, 2)), -0.2, 0.2), 0.05, 0.45),
        "obs_weight": jnp.clip(jnp.exp(math.log(4.0) - 2.0794415 * jax.random.uniform(part_splits[5], (L, NXC, NYC), jnp.float32) ** block_scale(part_splits[5], (L, NXC, NYC), ((0, 2), (1, 4), (2, 2)), -0.2, 0.2)), 0.5, 4.0),
    }


tent_weights = (0.125, 0.375, 0.375, 0.125)


def restrict_axis(values, offset, axis):
    length = values.shape[axis] - 4
    summed = jnp.zeros_like(lax.slice_in_dim(values, 0, length - 3, 4, axis))
    for position in range(4):
        window = lax.dynamic_slice_in_dim(values, (offset + position + 1).astype(jnp.int32), length - 3, axis)
        window = lax.slice_in_dim(window, 0, length - 3, 4, axis)
        summed = summed + tent_weights[position] * window
    return summed


def restrict_level(plane, offsets):
    padded = jnp.pad(plane.astype(jnp.float32), 2)
    rows_done = restrict_axis(padded, offsets[0], 0)
    return restrict_axis(rows_done, offsets[1], 1)


def prolong_axis(padded, offset, fine_len, axis):
    positions = jnp.arange(fine_len, dtype=jnp.int32) - offset.astype(jnp.int32)
    lower = jnp.floor_divide(positions, 4)
    upper_weight = (positions - 4 * lower).astype(jnp.float32) * 0.25
    first = jnp.take(padded, lower + 1, axis=axis)
    second = jnp.take(padded, lower + 2, axis=axis)
    shape = [1] * padded.ndim
    shape[axis] = fine_len
    upper_weight = upper_weight.reshape(shape)
    return (1.0 - upper_weight) * first + upper_weight * second


def prolong_level(plane, offsets):
    padded = jnp.pad(plane, 1)
    rows_done = prolong_axis(padded, offsets[0], NXF, 0)
    return prolong_axis(rows_done, offsets[1], NYF, 1)


def tangent_step(state, east_courant, north_courant):
    west = jnp.concatenate([jnp.zeros_like(state[:, :1, :]), state[:, :-1, :]], axis=1)
    south = jnp.concatenate([jnp.zeros_like(state[:, :, :1]), state[:, :, :-1]], axis=2)
    return (1.0 - east_courant - north_courant) * state + east_courant * west + north_courant * south


def adjoint_step(state, east_courant, north_courant):
    east_part = east_courant * state
    north_part = north_courant * state
    east_full = jnp.concatenate([east_part[:, 1:, :], jnp.zeros_like(east_part[:, :1, :])], axis=1)
    north_full = jnp.concatenate([north_part[:, :, 1:], jnp.zeros_like(north_part[:, :, :1])], axis=2)
    return (1.0 - east_courant - north_courant) * state + east_full + north_full


def reference(innovations, restrict_offsets, prolong_offsets, east_courant, north_courant, obs_weight):
    def restrict_time(plane_set):
        return jax.vmap(restrict_level)(plane_set, restrict_offsets)

    restricted = lax.map(restrict_time, innovations)
    adjoint_state = obs_weight * restricted[TS - 1]
    for time_index in range(TS - 2, -1, -1):
        adjoint_state = adjoint_step(adjoint_state, east_courant, north_courant) + obs_weight * restricted[time_index]
    gradient_rhs = adjoint_step(adjoint_state, east_courant, north_courant)

    solution = jnp.zeros_like(gradient_rhs)
    residual = gradient_rhs
    direction = gradient_rhs
    norm_now = jnp.sum(residual * residual)
    for iteration in range(ITERS):
        states = []
        state = direction
        for time_index in range(TS):
            state = tangent_step(state, east_courant, north_courant)
            states.append(state)
        adjoint_state = obs_weight * states[TS - 1]
        for time_index in range(TS - 2, -1, -1):
            adjoint_state = adjoint_step(adjoint_state, east_courant, north_courant) + obs_weight * states[time_index]
        image = direction + adjoint_step(adjoint_state, east_courant, north_courant)
        alpha = norm_now / jnp.sum(direction * image)
        solution = solution + alpha * direction
        residual = residual - alpha * image
        if iteration + 1 < ITERS:
            norm_next = jnp.sum(residual * residual)
            direction = residual + (norm_next / norm_now) * direction
            norm_now = norm_next
    increment_fine = jax.vmap(prolong_level)(solution, prolong_offsets)
    return increment_fine, residual
```

```python
import functools

import jax
import jax.numpy as jnp
from jax import lax
from jax.experimental import pallas as pl
from jax.experimental.pallas import tpu as pltpu
from jax.sharding import PartitionSpec as P

MESH = pl.DeviceIdType.MESH
HALO = 8
F32, BF16 = jnp.float32, jnp.bfloat16


def repeat(count, body):
    if count <= 16:
        for k in range(1, count):
            body(k)
    else:
        lax.fori_loop(1, count, lambda k, carry: (body(k), carry)[1], 0)


def split(values):
    high = values.astype(BF16)
    return high, (values - high.astype(F32)).astype(BF16)


def dot(a, b):
    return jnp.dot(a, b, preferred_element_type=F32)


def split_dot(values, weights):
    high, low = split(values)
    return dot(high, weights) + dot(low, weights)


def iota(shape, dim):
    return lax.broadcasted_iota(jnp.int32, shape, dim)


def kernel(
    sizes, inn, r_off, p_off, east, north, weight, out, res, coef, gx_in, gy_in, gx_out, gy_out,
    red, c_send, c_recv, g_send, g_recv, r_send, r_recv,
):
    nx, ny, nl = sizes
    group = nx * ny * nl
    steps, levels, fine_x, fine_y = inn.shape
    rows, cols = fine_x // 4, fine_y // 4
    ext = rows + 2 * HALO
    wide = 2 * cols
    ix, iy, il = lax.axis_index("gx"), lax.axis_index("gy"), lax.axis_index("lev")
    me = (ix * ny + iy) * nl + il

    def peer(k):
        other = lax.rem(me + k, group)
        return {
            "gx": other // (ny * nl),
            "gy": lax.rem(other // nl, ny),
            "lev": lax.rem(other, nl),
        }

    coef[...] = jnp.zeros_like(coef)
    gx_in[...] = jnp.zeros_like(gx_in)
    gy_in[...] = jnp.zeros_like(gy_in)
    for field, ref in enumerate((east, north, weight)):
        coef[0, field, :, HALO : HALO + rows, :] = ref[...]
    barrier = pltpu.get_barrier_semaphore()
    repeat(group, lambda k: pl.semaphore_signal(barrier, inc=1, device_id=peer(k), device_id_type=MESH))
    pl.semaphore_wait(barrier, group - 1)

    sides = [(dx, dy) for dx in (0, 1, -1) for dy in (0, 1, -1) if (dx, dy) != (0, 0)]
    sides = [(dx, dy) for dx, dy in sides if (nx > 1 or not dx) and (ny > 1 or not dy)]

    def present(dx, dy):
        x, y = ix + dx, iy + dy
        return (x >= 0) & (x < nx) & (y >= 0) & (y < ny)

    def remote(src, dst, send, recv, dx, dy):
        return pltpu.make_async_remote_copy(
            src_ref=src, dst_ref=dst, send_sem=send, recv_sem=recv,
            device_id={"gx": ix + dx, "gy": iy + dy}, device_id_type=MESH,
        )

    column = {0: 0, 1: 1, -1: 2}
    coef_rows = {1: (rows, 0, HALO), -1: (HALO, HALO + rows, HALO), 0: (HALO, HALO, rows)}
    half = ext // 2
    half_rows = {1: (half, 0, half), -1: (0, half, half), 0: (0, 0, ext)}

    def coef_copy(number, dx, dy):
        src, dst, size = coef_rows[dx]
        return remote(
            coef.at[0, :, :, pl.ds(src, size)], coef.at[column[dy], :, :, pl.ds(dst, size)],
            c_send.at[number], c_recv.at[number], dx, dy,
        )

    def g_copy(number, dx, dy):
        src, dst, size = half_rows[dx]
        if dy == 0:
            src_ref, dst_ref = gx_out.at[:, pl.ds(src, size)], gx_in.at[:, pl.ds(dst, size)]
        else:
            slot = column[dy] - 1
            src_ref = gy_out.at[slot, :, pl.ds(src, size)]
            dst_ref = gy_in.at[slot + (2 if dx else 0), :, pl.ds(dst, size)]
        return remote(src_ref, dst_ref, g_send.at[number], g_recv.at[number], dx, dy)

    def start_all(make):
        for number, (dx, dy) in enumerate(sides):
            @pl.when(present(dx, dy))
            def _():
                make(number, dx, dy).start()

    def wait_recv_all(make):
        for number, (dx, dy) in enumerate(sides):
            @pl.when(present(-dx, -dy))
            def _():
                make(number, dx, dy).wait_recv()

    def wait_send_all(make):
        for number, (dx, dy) in enumerate(sides):
            @pl.when(present(dx, dy))
            def _():
                make(number, dx, dy).wait_send()

    start_all(coef_copy)

    def wrapped(shape, dim):
        lane = iota(shape, dim)
        return jnp.where(lane < wide - wide // 4, lane, lane - wide)

    a_shape = (steps * ext, steps * fine_x)
    a_row, a_col = iota(a_shape, 0), iota(a_shape, 1)
    a_same = a_row // ext == a_col // fine_x
    a_base = 0.25 * (a_col % fine_x - 4 * (a_row % ext - HALO)).astype(F32)
    a_base = jnp.where(a_same, a_base, 1e6)
    c_shape = (fine_y, wide)
    c_base = 0.25 * (iota(c_shape, 0) - 4 * wrapped(c_shape, 1)).astype(F32)

    def tent(base, offset):
        return jnp.maximum(0.5 - jnp.abs(base - (offset.astype(F32) + 0.5) * 0.25), 0.0).astype(BF16)

    restricted = []
    for level in range(levels):
        fine = inn[:, level].reshape(steps * fine_x, fine_y)
        part = dot(tent(a_base, r_off[level, 0]), fine)
        restricted.append(split_dot(part, tent(c_base, r_off[level, 1])))

    def at_time(t):
        return jnp.concatenate([r[t * ext : (t + 1) * ext] for r in restricted], axis=0)

    wait_recv_all(coef_copy)
    lane = iota((levels * ext, cols), 1)
    low, high = lane < HALO, lane >= cols - HALO

    def extended(field):
        own, left, right = (coef[c, field].reshape(levels * ext, cols) for c in range(3))
        rim = jnp.where(low, right, jnp.where(high, left, 0.0))
        return jnp.concatenate([own, rim], axis=1)

    e, n, w_obs = extended(0), extended(1), extended(2)
    stay = 1.0 - e - n
    total_rows = levels * ext

    def forward(x):
        return stay * x + e * pltpu.roll(x, 1, 0) + n * pltpu.roll(x, 1, 1)

    def adjoint(y):
        return stay * y + pltpu.roll(e * y, total_rows - 1, 0) + pltpu.roll(n * y, wide - 1, 1)

    lam = w_obs * at_time(steps - 1)
    for t in range(steps - 2, -1, -1):
        lam = adjoint(lam) + w_obs * at_time(t)
    mine = adjoint(lam)
    near, far = mine[:, :cols], mine[:, cols:]
    gx_out[...] = mine.reshape(levels, ext, wide)
    gy_out[0] = jnp.where(low, far, near).reshape(levels, ext, cols)
    gy_out[1] = jnp.where(low, near, far).reshape(levels, ext, cols)
    start_all(g_copy)

    m_shape = (total_rows, wide)
    m_row = iota(m_shape, 0) % ext - HALO + ix * rows
    m_col = wrapped(m_shape, 1) + iy * cols
    inside = (m_row >= 0) & (m_row < nx * rows) & (m_col >= 0) & (m_col < ny * cols)

    wait_recv_all(g_copy)
    from_left = (gy_in[0] + gy_in[2]).reshape(total_rows, cols)
    from_right = (gy_in[1] + gy_in[3]).reshape(total_rows, cols)
    near_rim = jnp.where(low, from_left, jnp.where(high, from_right, 0.0))
    far_rim = jnp.where(low, from_right, jnp.where(high, from_left, 0.0))
    beside = gx_in[...].reshape(total_rows, wide)
    g = mine + beside + jnp.concatenate([near_rim, far_rim], axis=1)
    g = jnp.where(inside, g, 0.0)

    def hessian(p):
        states = []
        state = p
        for _ in range(steps):
            state = forward(state)
            states.append(state)
        lam = w_obs * states[-1]
        for t in range(steps - 2, -1, -1):
            lam = adjoint(lam) + w_obs * states[t]
        return p + adjoint(lam)

    w = jnp.where(inside, hessian(g), 0.0)
    v = hessian(w)

    def own(x):
        return [x[l * ext + HALO : l * ext + HALO + rows, :cols] for l in range(levels)]

    g_own, w_own, v_own = own(g), own(w), own(v)

    def partial(a, b):
        return sum(jnp.sum(x * y, axis=0, keepdims=True) for x, y in zip(a, b))

    gram = jnp.concatenate(
        [partial(g_own, g_own), partial(g_own, w_own), partial(w_own, w_own), partial(w_own, v_own)]
        + [jnp.zeros((4, cols), F32)], axis=0,
    )
    red[me] = gram

    def red_send(k):
        return pltpu.make_async_remote_copy(
            src_ref=red.at[me], dst_ref=red.at[me], send_sem=r_send.at[k], recv_sem=r_recv.at[me],
            device_id=peer(k), device_id_type=MESH,
        )

    def red_recv(k):
        other = lax.rem(me + k, group)
        return pltpu.make_async_remote_copy(
            src_ref=red.at[me], dst_ref=red.at[other], send_sem=r_send.at[k],
            recv_sem=r_recv.at[other], device_id=peer(k), device_id_type=MESH,
        )

    repeat(group, lambda k: red_send(k).start())

    q_shape = (wide, fine_y)
    q_base = 0.25 * iota(q_shape, 1).astype(F32) - wrapped(q_shape, 0).astype(F32)
    b_shape = (fine_x, 2 * ext)
    b_base = 0.25 * iota(b_shape, 0).astype(F32) - (iota(b_shape, 1) % ext - HALO).astype(F32)

    def hat(base, offset):
        return jnp.maximum(1.0 - jnp.abs(base - offset.astype(F32) * 0.25), 0.0).astype(BF16)

    fine_parts = []
    for level in range(levels):
        both = jnp.concatenate([x[level * ext : (level + 1) * ext] for x in (g, w)], axis=0)
        across = split_dot(both, hat(q_base, p_off[level, 1]))
        up = hat(b_base, p_off[level, 0])
        fine_parts.append([
            dot(up, jnp.concatenate(split(across[k * ext : (k + 1) * ext]), axis=0)) for k in range(2)
        ])

    repeat(group, lambda k: red_recv(k).wait_recv())
    sums = jnp.sum(jnp.sum(red[...], axis=0), axis=1, keepdims=True)
    gg, gw, ww, wv = (sums[k : k + 1] for k in range(4))
    alpha = gg / gw
    rr = gg - 2.0 * alpha * gw + alpha * alpha * ww
    beta = rr / gg
    more = 1.0 + beta
    curvature = more * more * gw - 2.0 * alpha * more * ww + alpha * alpha * wv
    alpha_1 = rr / curvature
    from_g = alpha + alpha_1 * more
    from_w = -alpha_1 * alpha
    res_w = -(alpha + alpha_1 * more)
    res_v = alpha_1 * alpha
    for level in range(levels):
        out[level] = from_g * fine_parts[level][0] + from_w * fine_parts[level][1]
        res[level] = g_own[level] + res_w * w_own[level] + res_v * v_own[level]

    wait_send_all(coef_copy)
    wait_send_all(g_copy)
    repeat(group, lambda k: red_send(k).wait_send())


def on_device(sizes, innovations, restrict_offsets, prolong_offsets, east, north, weight):
    _, levels, fine_x, fine_y = innovations.shape
    rows, cols = fine_x // 4, fine_y // 4
    ext = rows + 2 * HALO
    group = sizes[0] * sizes[1] * sizes[2]
    vmem = pl.BlockSpec(memory_space=pltpu.VMEM)
    smem = pl.BlockSpec(memory_space=pltpu.SMEM)
    dma = pltpu.SemaphoreType.DMA
    return pl.pallas_call(
        functools.partial(kernel, sizes),
        out_shape=(
            jax.ShapeDtypeStruct((levels, fine_x, fine_y), F32),
            jax.ShapeDtypeStruct((levels, rows, cols), F32),
        ),
        in_specs=[vmem, smem, smem, vmem, vmem, vmem],
        out_specs=(vmem, vmem),
        scratch_shapes=[
            pltpu.VMEM((3, 3, levels, ext, cols), F32),
            pltpu.VMEM((levels, ext, 2 * cols), F32),
            pltpu.VMEM((4, levels, ext, cols), F32),
            pltpu.VMEM((levels, ext, 2 * cols), F32),
            pltpu.VMEM((2, levels, ext, cols), F32),
            pltpu.VMEM((group, 8, cols), F32),
            dma((8,)), dma((8,)), dma((8,)), dma((8,)), dma((group,)), dma((group,)),
        ],
        compiler_params=pltpu.CompilerParams(
            collective_id=0, has_side_effects=True, vmem_limit_bytes=32 * 1024 * 1024
        ),
    )(innovations, restrict_offsets, prolong_offsets, east, north, weight)


def solution(mesh):
    sizes = tuple(mesh.shape[axis] for axis in ("gx", "gy", "lev"))
    inner = P(("ens", "lev"), "gx", "gy")
    in_specs = (P("ens", "lev", "gx", "gy"), P("lev", None), P("lev", None), inner, inner, inner)
    return jax.shard_map(
        functools.partial(on_device, sizes), mesh=mesh, in_specs=in_specs,
        out_specs=(inner, inner), check_vma=False,
    )
```

```python
import functools

import jax
import jax.numpy as jnp
from jax import lax
from jax.experimental import pallas as pl
from jax.experimental.pallas import tpu as pltpu
from jax.sharding import PartitionSpec as P

MESH = pl.DeviceIdType.MESH
HALO = 8
F32, BF16 = jnp.float32, jnp.bfloat16


def repeat(count, body):
    if count <= 16:
        for k in range(1, count):
            body(k)
    else:
        lax.fori_loop(1, count, lambda k, carry: (body(k), carry)[1], 0)


def split(values):
    high = values.astype(BF16)
    return high, (values - high.astype(F32)).astype(BF16)


def dot(a, b):
    return jnp.dot(a, b, preferred_element_type=F32)


def split_dot(values, weights):
    high, low = split(values)
    return dot(high, weights) + dot(low, weights)


def iota(shape, dim):
    return lax.broadcasted_iota(jnp.int32, shape, dim)


def kernel(
    sizes, inn_hbm, r_hbm, p_hbm, east, north, weight, out, res, inn, r_off, p_off, coef, gx_in, gy_in, gx_out, gy_out,
    red, local, c_send, c_recv, g_send, g_recv, r_send, r_recv,
):
    nx, ny, nl = sizes
    group = nx * ny * nl
    steps, levels, fine_x, fine_y = inn.shape
    rows, cols = fine_x // 4, fine_y // 4
    ext = rows + 2 * HALO
    wide = 2 * cols
    ix, iy, il = lax.axis_index("gx"), lax.axis_index("gy"), lax.axis_index("lev")
    me = (ix * ny + iy) * nl + il

    def peer(k):
        other = lax.rem(me + k, group)
        return {
            "gx": other // (ny * nl),
            "gy": lax.rem(other // nl, ny),
            "lev": lax.rem(other, nl),
        }

    loads = [
        pltpu.make_async_copy(src, dst, local.at[k])
        for k, (src, dst) in enumerate(
            [(ref, coef.at[0, field, :, pl.ds(HALO, rows)]) for field, ref in enumerate((east, north, weight))]
            + [(r_hbm, r_off), (inn_hbm, inn), (p_hbm, p_off)]
        )
    ]
    for load in loads:
        load.start()
    edge = jnp.zeros((3, levels, HALO, cols), F32)
    coef[0, :, :, :HALO] = edge
    coef[0, :, :, HALO + rows :] = edge
    coef[1:] = jnp.zeros((2, 3, levels, ext, cols), F32)
    gx_in[...] = jnp.zeros_like(gx_in)
    gy_in[...] = jnp.zeros_like(gy_in)
    barrier = pltpu.get_barrier_semaphore()
    repeat(group, lambda k: pl.semaphore_signal(barrier, inc=1, device_id=peer(k), device_id_type=MESH))
    def wrapped(shape, dim):
        lane = iota(shape, dim)
        return jnp.where(lane < wide - wide // 4, lane, lane - wide)

    a_shape = (steps * ext, steps * fine_x)
    a_row, a_col = iota(a_shape, 0), iota(a_shape, 1)
    a_same = a_row // ext == a_col // fine_x
    a_base = 0.25 * (a_col % fine_x - 4 * (a_row % ext - HALO)).astype(F32)
    a_base = jnp.where(a_same, a_base, 1e6)
    c_shape = (fine_y, wide)
    c_base = 0.25 * (iota(c_shape, 0) - 4 * wrapped(c_shape, 1)).astype(F32)

    def tent(base, offset):
        return jnp.maximum(0.5 - jnp.abs(base - (offset.astype(F32) + 0.5) * 0.25), 0.0).astype(BF16)

    loads[3].wait()
    a_mats = [tent(a_base, r_off[level, 0]) for level in range(levels)]
    c_mats = [tent(c_base, r_off[level, 1]) for level in range(levels)]

    pl.semaphore_wait(barrier, group - 1)
    for load in loads[:3]:
        load.wait()

    sides = [(dx, dy) for dx in (0, 1, -1) for dy in (0, 1, -1) if (dx, dy) != (0, 0)]
    sides = [(dx, dy) for dx, dy in sides if (nx > 1 or not dx) and (ny > 1 or not dy)]

    def present(dx, dy):
        x, y = ix + dx, iy + dy
        return (x >= 0) & (x < nx) & (y >= 0) & (y < ny)

    def remote(src, dst, send, recv, dx, dy):
        return pltpu.make_async_remote_copy(
            src_ref=src, dst_ref=dst, send_sem=send, recv_sem=recv,
            device_id={"gx": ix + dx, "gy": iy + dy}, device_id_type=MESH,
        )

    column = {0: 0, 1: 1, -1: 2}
    coef_rows = {1: (rows, 0, HALO), -1: (HALO, HALO + rows, HALO), 0: (HALO, HALO, rows)}
    half = ext // 2
    half_rows = {1: (half, 0, half), -1: (0, half, half), 0: (0, 0, ext)}

    def coef_copy(number, dx, dy):
        src, dst, size = coef_rows[dx]
        return remote(
            coef.at[0, :, :, pl.ds(src, size)], coef.at[column[dy], :, :, pl.ds(dst, size)],
            c_send.at[number], c_recv.at[number], dx, dy,
        )

    def g_copy(number, dx, dy):
        src, dst, size = half_rows[dx]
        if dy == 0:
            src_ref, dst_ref = gx_out.at[:, pl.ds(src, size)], gx_in.at[:, pl.ds(dst, size)]
        else:
            slot = column[dy] - 1
            src_ref = gy_out.at[slot, :, pl.ds(src, size)]
            dst_ref = gy_in.at[slot + (2 if dx else 0), :, pl.ds(dst, size)]
        return remote(src_ref, dst_ref, g_send.at[number], g_recv.at[number], dx, dy)

    def start_all(make):
        for number, (dx, dy) in enumerate(sides):
            @pl.when(present(dx, dy))
            def _():
                make(number, dx, dy).start()

    def wait_recv_all(make):
        for number, (dx, dy) in enumerate(sides):
            @pl.when(present(-dx, -dy))
            def _():
                make(number, dx, dy).wait_recv()

    def wait_send_all(make):
        for number, (dx, dy) in enumerate(sides):
            @pl.when(present(dx, dy))
            def _():
                make(number, dx, dy).wait_send()

    start_all(coef_copy)

    loads[4].wait()
    restricted = []
    for level in range(levels):
        fine = inn[:, level].reshape(steps * fine_x, fine_y)
        part = dot(a_mats[level], fine)
        restricted.append(split_dot(part, c_mats[level]))

    def at_time(t):
        return jnp.concatenate([r[t * ext : (t + 1) * ext] for r in restricted], axis=0)

    wait_recv_all(coef_copy)
    lane = iota((levels * ext, cols), 1)
    low, high = lane < HALO, lane >= cols - HALO

    def extended(field):
        own, left, right = (coef[c, field].reshape(levels * ext, cols) for c in range(3))
        rim = jnp.where(low, right, jnp.where(high, left, 0.0))
        return jnp.concatenate([own, rim], axis=1)

    e, n, w_obs = extended(0), extended(1), extended(2)
    stay = 1.0 - e - n
    total_rows = levels * ext

    def forward(x):
        return stay * x + e * pltpu.roll(x, 1, 0) + n * pltpu.roll(x, 1, 1)

    def adjoint(y):
        return stay * y + pltpu.roll(e * y, total_rows - 1, 0) + pltpu.roll(n * y, wide - 1, 1)

    lam = w_obs * at_time(steps - 1)
    for t in range(steps - 2, -1, -1):
        lam = adjoint(lam) + w_obs * at_time(t)
    mine = adjoint(lam)
    near, far = mine[:, :cols], mine[:, cols:]
    gx_out[...] = mine.reshape(levels, ext, wide)
    gy_out[0] = jnp.where(low, far, near).reshape(levels, ext, cols)
    gy_out[1] = jnp.where(low, near, far).reshape(levels, ext, cols)
    start_all(g_copy)

    m_shape = (total_rows, wide)
    m_row = iota(m_shape, 0) % ext - HALO + ix * rows
    m_col = wrapped(m_shape, 1) + iy * cols
    inside = (m_row >= 0) & (m_row < nx * rows) & (m_col >= 0) & (m_col < ny * cols)

    wait_recv_all(g_copy)
    from_left = (gy_in[0] + gy_in[2]).reshape(total_rows, cols)
    from_right = (gy_in[1] + gy_in[3]).reshape(total_rows, cols)
    near_rim = jnp.where(low, from_left, jnp.where(high, from_right, 0.0))
    far_rim = jnp.where(low, from_right, jnp.where(high, from_left, 0.0))
    beside = gx_in[...].reshape(total_rows, wide)
    g = mine + beside + jnp.concatenate([near_rim, far_rim], axis=1)
    g = jnp.where(inside, g, 0.0)

    def hessian(p):
        states = []
        state = p
        for _ in range(steps):
            state = forward(state)
            states.append(state)
        lam = w_obs * states[-1]
        for t in range(steps - 2, -1, -1):
            lam = adjoint(lam) + w_obs * states[t]
        return p + adjoint(lam)

    w = jnp.where(inside, hessian(g), 0.0)
    v = hessian(w)

    def own(x):
        return [x[l * ext + HALO : l * ext + HALO + rows, :cols] for l in range(levels)]

    g_own, w_own, v_own = own(g), own(w), own(v)

    def partial(a, b):
        return sum(jnp.sum(x * y, axis=0, keepdims=True) for x, y in zip(a, b))

    gram = jnp.concatenate(
        [partial(g_own, g_own), partial(g_own, w_own), partial(w_own, w_own), partial(w_own, v_own)]
        + [jnp.zeros((4, cols), F32)], axis=0,
    )
    red[me] = gram

    def red_send(k):
        return pltpu.make_async_remote_copy(
            src_ref=red.at[me], dst_ref=red.at[me], send_sem=r_send.at[k], recv_sem=r_recv.at[me],
            device_id=peer(k), device_id_type=MESH,
        )

    def red_recv(k):
        other = lax.rem(me + k, group)
        return pltpu.make_async_remote_copy(
            src_ref=red.at[me], dst_ref=red.at[other], send_sem=r_send.at[k],
            recv_sem=r_recv.at[other], device_id=peer(k), device_id_type=MESH,
        )

    repeat(group, lambda k: red_send(k).start())

    q_shape = (wide, fine_y)
    q_base = 0.25 * iota(q_shape, 1).astype(F32) - wrapped(q_shape, 0).astype(F32)
    b_shape = (fine_x, 2 * ext)
    b_base = 0.25 * iota(b_shape, 0).astype(F32) - (iota(b_shape, 1) % ext - HALO).astype(F32)

    def hat(base, offset):
        return jnp.maximum(1.0 - jnp.abs(base - offset.astype(F32) * 0.25), 0.0).astype(BF16)

    loads[5].wait()
    fine_parts = []
    for level in range(levels):
        both = jnp.concatenate([x[level * ext : (level + 1) * ext] for x in (g, w)], axis=0)
        across = split_dot(both, hat(q_base, p_off[level, 1]))
        up = hat(b_base, p_off[level, 0])
        fine_parts.append([
            dot(up, jnp.concatenate(split(across[k * ext : (k + 1) * ext]), axis=0)) for k in range(2)
        ])

    repeat(group, lambda k: red_recv(k).wait_recv())
    sums = jnp.sum(jnp.sum(red[...], axis=0), axis=1, keepdims=True)
    gg, gw, ww, wv = (sums[k : k + 1] for k in range(4))
    alpha = gg / gw
    rr = gg - 2.0 * alpha * gw + alpha * alpha * ww
    beta = rr / gg
    more = 1.0 + beta
    curvature = more * more * gw - 2.0 * alpha * more * ww + alpha * alpha * wv
    alpha_1 = rr / curvature
    from_g = alpha + alpha_1 * more
    from_w = -alpha_1 * alpha
    res_w = -(alpha + alpha_1 * more)
    res_v = alpha_1 * alpha
    for level in range(levels):
        out[level] = from_g * fine_parts[level][0] + from_w * fine_parts[level][1]
        res[level] = g_own[level] + res_w * w_own[level] + res_v * v_own[level]

    wait_send_all(coef_copy)
    wait_send_all(g_copy)
    repeat(group, lambda k: red_send(k).wait_send())


def on_device(sizes, innovations, restrict_offsets, prolong_offsets, east, north, weight):
    _, levels, fine_x, fine_y = innovations.shape
    rows, cols = fine_x // 4, fine_y // 4
    ext = rows + 2 * HALO
    group = sizes[0] * sizes[1] * sizes[2]
    vmem = pl.BlockSpec(memory_space=pltpu.VMEM)
    hbm = pl.BlockSpec(memory_space=pltpu.HBM)
    dma = pltpu.SemaphoreType.DMA
    return pl.pallas_call(
        functools.partial(kernel, sizes),
        out_shape=(
            jax.ShapeDtypeStruct((levels, fine_x, fine_y), F32),
            jax.ShapeDtypeStruct((levels, rows, cols), F32),
        ),
        in_specs=[hbm] * 6,
        out_specs=(vmem, vmem),
        scratch_shapes=[
            pltpu.VMEM(innovations.shape, BF16),
            pltpu.SMEM((levels, 2), jnp.int32),
            pltpu.SMEM((levels, 2), jnp.int32),
            pltpu.VMEM((3, 3, levels, ext, cols), F32),
            pltpu.VMEM((levels, ext, 2 * cols), F32),
            pltpu.VMEM((4, levels, ext, cols), F32),
            pltpu.VMEM((levels, ext, 2 * cols), F32),
            pltpu.VMEM((2, levels, ext, cols), F32),
            pltpu.VMEM((group, 8, cols), F32),
            dma((6,)), dma((8,)), dma((8,)), dma((8,)), dma((8,)), dma((group,)), dma((group,)),
        ],
        compiler_params=pltpu.CompilerParams(
            collective_id=0, has_side_effects=True, vmem_limit_bytes=32 * 1024 * 1024
        ),
    )(innovations, restrict_offsets, prolong_offsets, east, north, weight)


def solution(mesh):
    sizes = tuple(mesh.shape[axis] for axis in ("gx", "gy", "lev"))
    inner = P(("ens", "lev"), "gx", "gy")
    in_specs = (P("ens", "lev", "gx", "gy"), P("lev", None), P("lev", None), inner, inner, inner)
    return jax.shard_map(
        functools.partial(on_device, sizes), mesh=mesh, in_specs=in_specs,
        out_specs=(inner, inner), check_vma=False,
    )
```

```python
import functools

import jax
import jax.numpy as jnp
from jax import lax
from jax.experimental import pallas as pl
from jax.experimental.pallas import tpu as pltpu
from jax.sharding import PartitionSpec as P

MESH = pl.DeviceIdType.MESH
HALO = 8
SIDES = tuple((dx, dy) for dx in (0, 1, -1) for dy in (0, 1, -1) if dx or dy)
F32, BF16 = jnp.float32, jnp.bfloat16


def repeat(count, body):
    if count <= 16:
        for k in range(1, count):
            body(k)
    else:
        lax.fori_loop(1, count, lambda k, carry: (body(k), carry)[1], 0)


def split(values):
    high = values.astype(BF16)
    return high, (values - high.astype(F32)).astype(BF16)


def dot(a, b):
    return jnp.dot(a, b, preferred_element_type=F32)


def split_dot(values, weights):
    high, low = split(values)
    return dot(high, weights) + dot(low, weights)


def iota(shape, dim):
    return lax.broadcasted_iota(jnp.int32, shape, dim)


def kernel(
    sizes, inn_hbm, r_hbm, p_hbm, east, north, weight, out, res, inn, r_off, p_off, coef, c_rim, c_pack, g_near, g_rim, g_pack, near_out,
    red, local, c_send, c_recv, g_send, g_recv, r_send, r_recv,
):
    nx, ny, nl = sizes
    group = nx * ny * nl
    steps, levels, fine_x, fine_y = inn.shape
    rows, cols = fine_x // 4, fine_y // 4
    ext = rows + 2 * HALO
    wide = 2 * cols
    ix, iy, il = lax.axis_index("gx"), lax.axis_index("gy"), lax.axis_index("lev")
    me = (ix * ny + iy) * nl + il

    def peer(k):
        other = lax.rem(me + k, group)
        return {
            "gx": other // (ny * nl),
            "gy": lax.rem(other // nl, ny),
            "lev": lax.rem(other, nl),
        }

    loads = [
        pltpu.make_async_copy(src, dst, local.at[k])
        for k, (src, dst) in enumerate(
            [(ref, coef.at[field, :, pl.ds(HALO, rows)]) for field, ref in enumerate((east, north, weight))]
            + [(r_hbm, r_off), (inn_hbm, inn), (p_hbm, p_off)]
        )
    ]
    for load in loads:
        load.start()
    edge = jnp.zeros((3, levels, HALO, cols), F32)
    coef[:, :, :HALO] = edge
    coef[:, :, HALO + rows :] = edge
    for ref in (c_rim, g_near, g_rim):
        ref[...] = jnp.zeros_like(ref)
    barrier = pltpu.get_barrier_semaphore()
    repeat(group, lambda k: pl.semaphore_signal(barrier, inc=1, device_id=peer(k), device_id_type=MESH))
    def wrapped(shape, dim):
        lane = iota(shape, dim)
        return jnp.where(lane < wide - wide // 4, lane, lane - wide)

    a_shape = (steps * ext, steps * fine_x)
    a_row, a_col = iota(a_shape, 0), iota(a_shape, 1)
    a_same = a_row // ext == a_col // fine_x
    a_base = 0.25 * (a_col % fine_x - 4 * (a_row % ext - HALO)).astype(F32)
    a_base = jnp.where(a_same, a_base, 1e6)
    c_shape = (fine_y, wide)
    c_base = 0.25 * (iota(c_shape, 0) - 4 * wrapped(c_shape, 1)).astype(F32)

    def tent(base, offset):
        return jnp.maximum(0.5 - jnp.abs(base - (offset.astype(F32) + 0.5) * 0.25), 0.0).astype(BF16)

    loads[3].wait()
    a_mats = [tent(a_base, r_off[level, 0]) for level in range(levels)]
    c_mats = [tent(c_base, r_off[level, 1]) for level in range(levels)]

    pl.semaphore_wait(barrier, group - 1)
    for load in loads[:3]:
        load.wait()

    def present(dx, dy):
        x, y = ix + dx, iy + dy
        return (x >= 0) & (x < nx) & (y >= 0) & (y < ny)

    def remote(src, dst, send, recv, dx, dy):
        return pltpu.make_async_remote_copy(
            src_ref=src, dst_ref=dst, send_sem=send, recv_sem=recv,
            device_id={"gx": ix + dx, "gy": iy + dy}, device_id_type=MESH,
        )

    half = ext // 2
    coef_rows = {1: (rows, 0), -1: (HALO, HALO + rows)}
    half_rows = {1: (half, 0), -1: (0, half)}

    def coef_copies(number, dx, dy):
        sems = c_send.at[number], c_recv.at[number]
        if dy:
            return [remote(c_pack, c_rim.at[number], *sems, dx, dy)]
        src, dst = coef_rows[dx]
        return [remote(coef.at[:, :, pl.ds(src, HALO)], coef.at[:, :, pl.ds(dst, HALO)], *sems, dx, dy)]

    def g_copies(number, dx, dy):
        slot = {1: 0, -1: 1, 0: 2}[dy]
        found = [remote(g_pack.at[slot], g_rim.at[number], g_send.at[number], g_recv.at[number], dx, dy)]
        if dy == 0:
            src, dst = half_rows[dx]
            extra = len(SIDES) + number
            found.append(remote(
                near_out.at[:, pl.ds(src, half)], g_near.at[:, pl.ds(dst, half)],
                g_send.at[extra], g_recv.at[extra], dx, dy,
            ))
        return found

    def start_all(make):
        for number, (dx, dy) in enumerate(SIDES):
            @pl.when(present(dx, dy))
            def _():
                for copy in make(number, dx, dy):
                    copy.start()

    def wait_recv_all(make):
        for number, (dx, dy) in enumerate(SIDES):
            @pl.when(present(-dx, -dy))
            def _():
                for copy in make(number, dx, dy):
                    copy.wait_recv()

    def wait_send_all(make):
        for number, (dx, dy) in enumerate(SIDES):
            @pl.when(present(dx, dy))
            def _():
                for copy in make(number, dx, dy):
                    copy.wait_send()

    tile_lane = iota((HALO, cols), 1)
    window = (tile_lane + HALO) // (2 * HALO) % (cols // (2 * HALO))
    upper = (tile_lane + HALO) % (2 * HALO) < HALO

    def turn(tile, windows):
        shift = windows * 2 * HALO % cols
        return pltpu.roll(tile, shift, 1) if shift else tile

    def pack(tiles):
        packed = jnp.zeros((HALO, cols), F32)
        for k, tile in enumerate(tiles):
            packed = jnp.where(window == k, turn(tile, k), packed)
        return packed

    def unpack(packed, k):
        return jnp.where(window == 0, turn(packed, -k), 0.0)

    row_tiles = rows // HALO

    def own_tiles(field):
        return [
            coef[field, level, HALO * (1 + r) : HALO * (2 + r), :]
            for level in range(levels) for r in range(row_tiles)
        ]

    c_pack[0] = pack(own_tiles(0) + own_tiles(1))
    c_pack[1] = pack(own_tiles(2))

    def arrived(dx, dy):
        return SIDES.index((-dx, -dy))

    start_all(coef_copies)

    loads[4].wait()
    restricted = []
    for level in range(levels):
        fine = inn[:, level].reshape(steps * fine_x, fine_y)
        part = dot(a_mats[level], fine)
        restricted.append(split_dot(part, c_mats[level]))

    def at_time(t):
        return jnp.concatenate([r[t * ext : (t + 1) * ext] for r in restricted], axis=0)

    wait_recv_all(coef_copies)
    rims = [
        jnp.where(upper, c_rim[arrived(dx, -1)], c_rim[arrived(dx, 1)]) for dx in (-1, 0, 1)
    ]

    def extended(field):
        part, first = field // 2, field % 2 * levels * row_tiles
        far_tiles = []
        for level in range(levels):
            k = first + level * row_tiles
            far_tiles.append(unpack(rims[0][part], k + row_tiles - 1))
            far_tiles += [unpack(rims[1][part], k + r) for r in range(row_tiles)]
            far_tiles.append(unpack(rims[2][part], k))
        near = coef[field].reshape(levels * ext, cols)
        return jnp.concatenate([near, jnp.concatenate(far_tiles, axis=0)], axis=1)

    e, n, w_obs = extended(0), extended(1), extended(2)
    stay = 1.0 - e - n
    total_rows = levels * ext

    def forward(x):
        return stay * x + e * pltpu.roll(x, 1, 0) + n * pltpu.roll(x, 1, 1)

    def adjoint(y):
        return stay * y + pltpu.roll(e * y, total_rows - 1, 0) + pltpu.roll(n * y, wide - 1, 1)

    lam = w_obs * at_time(steps - 1)
    for t in range(steps - 2, -1, -1):
        lam = adjoint(lam) + w_obs * at_time(t)
    mine = adjoint(lam)
    near, far = mine[:, :cols], mine[:, cols:]
    tiles = total_rows // HALO
    near_pack = pack([near[HALO * k : HALO * (k + 1)] for k in range(tiles)])
    far_pack = pack([far[HALO * k : HALO * (k + 1)] for k in range(tiles)])
    g_pack[0] = jnp.where(upper, near_pack, far_pack)
    g_pack[1] = jnp.where(upper, far_pack, near_pack)
    g_pack[2] = far_pack
    near_out[...] = near.reshape(levels, ext, cols)
    start_all(g_copies)

    m_shape = (total_rows, wide)
    m_row = iota(m_shape, 0) % ext - HALO + ix * rows
    m_col = wrapped(m_shape, 1) + iy * cols
    inside = (m_row >= 0) & (m_row < nx * rows) & (m_col >= 0) & (m_col < ny * cols)

    wait_recv_all(g_copies)
    ext_tiles = ext // HALO
    first_half = window % ext_tiles < ext_tiles // 2

    def shifted(dy):
        back = turn(g_rim[arrived(-1, dy)], -(ext_tiles // 2))
        ahead = turn(g_rim[arrived(1, dy)], ext_tiles // 2)
        return jnp.where(first_half, back, ahead)

    from_left = g_rim[arrived(0, -1)] + shifted(-1)
    from_right = g_rim[arrived(0, 1)] + shifted(1)
    near_rim = jnp.where(upper, from_right, from_left)
    far_rim = jnp.where(upper, from_left, from_right) + shifted(0)

    def unpack_all(packed):
        return jnp.concatenate([unpack(packed, k) for k in range(tiles)], axis=0)

    beside = g_near[...].reshape(total_rows, cols)
    g = mine + jnp.concatenate([beside + unpack_all(near_rim), unpack_all(far_rim)], axis=1)
    g = jnp.where(inside, g, 0.0)

    def hessian(p):
        states = []
        state = p
        for _ in range(steps):
            state = forward(state)
            states.append(state)
        lam = w_obs * states[-1]
        for t in range(steps - 2, -1, -1):
            lam = adjoint(lam) + w_obs * states[t]
        return p + adjoint(lam)

    w = jnp.where(inside, hessian(g), 0.0)
    v = hessian(w)

    def own(x):
        return [x[l * ext + HALO : l * ext + HALO + rows, :cols] for l in range(levels)]

    g_own, w_own, v_own = own(g), own(w), own(v)

    def partial(a, b):
        return sum(jnp.sum(x * y, axis=0, keepdims=True) for x, y in zip(a, b))

    gram = jnp.concatenate(
        [partial(g_own, g_own), partial(g_own, w_own), partial(w_own, w_own), partial(w_own, v_own)]
        + [jnp.zeros((4, cols), F32)], axis=0,
    )
    spread = jnp.sum(gram, axis=1, keepdims=True)
    quarter = iota((8, cols), 1) // (cols // 4)
    red[me] = jnp.sum(jnp.where(quarter == iota((8, cols), 0), spread, 0.0), axis=0, keepdims=True)

    def red_send(k):
        return pltpu.make_async_remote_copy(
            src_ref=red.at[me], dst_ref=red.at[me], send_sem=r_send.at[k], recv_sem=r_recv.at[me],
            device_id=peer(k), device_id_type=MESH,
        )

    def red_recv(k):
        other = lax.rem(me + k, group)
        return pltpu.make_async_remote_copy(
            src_ref=red.at[me], dst_ref=red.at[other], send_sem=r_send.at[k],
            recv_sem=r_recv.at[other], device_id=peer(k), device_id_type=MESH,
        )

    repeat(group, lambda k: red_send(k).start())

    q_shape = (wide, fine_y)
    q_base = 0.25 * iota(q_shape, 1).astype(F32) - wrapped(q_shape, 0).astype(F32)
    b_shape = (fine_x, 2 * ext)
    b_base = 0.25 * iota(b_shape, 0).astype(F32) - (iota(b_shape, 1) % ext - HALO).astype(F32)

    def hat(base, offset):
        return jnp.maximum(1.0 - jnp.abs(base - offset.astype(F32) * 0.25), 0.0).astype(BF16)

    loads[5].wait()
    fine_parts = []
    for level in range(levels):
        both = jnp.concatenate([x[level * ext : (level + 1) * ext] for x in (g, w)], axis=0)
        across = split_dot(both, hat(q_base, p_off[level, 1]))
        up = hat(b_base, p_off[level, 0])
        fine_parts.append([
            dot(up, jnp.concatenate(split(across[k * ext : (k + 1) * ext]), axis=0)) for k in range(2)
        ])

    repeat(group, lambda k: red_recv(k).wait_recv())
    sums = jnp.sum(red[...], axis=0)
    gg, gw, ww, wv = (sums[:, k * (cols // 4)][:, None] for k in range(4))
    alpha = gg / gw
    rr = gg - 2.0 * alpha * gw + alpha * alpha * ww
    beta = rr / gg
    more = 1.0 + beta
    curvature = more * more * gw - 2.0 * alpha * more * ww + alpha * alpha * wv
    alpha_1 = rr / curvature
    from_g = alpha + alpha_1 * more
    from_w = -alpha_1 * alpha
    res_w = -(alpha + alpha_1 * more)
    res_v = alpha_1 * alpha
    for level in range(levels):
        out[level] = from_g * fine_parts[level][0] + from_w * fine_parts[level][1]
        res[level] = g_own[level] + res_w * w_own[level] + res_v * v_own[level]

    wait_send_all(coef_copies)
    wait_send_all(g_copies)
    repeat(group, lambda k: red_send(k).wait_send())


def on_device(sizes, innovations, restrict_offsets, prolong_offsets, east, north, weight):
    _, levels, fine_x, fine_y = innovations.shape
    rows, cols = fine_x // 4, fine_y // 4
    ext = rows + 2 * HALO
    group = sizes[0] * sizes[1] * sizes[2]
    vmem = pl.BlockSpec(memory_space=pltpu.VMEM)
    hbm = pl.BlockSpec(memory_space=pltpu.HBM)
    dma = pltpu.SemaphoreType.DMA
    return pl.pallas_call(
        functools.partial(kernel, sizes),
        out_shape=(
            pltpu.VMEM((levels, fine_x, fine_y), F32),
            pltpu.VMEM((levels, rows, cols), F32),
        ),
        in_specs=[hbm] * 6,
        out_specs=(vmem, vmem),
        scratch_shapes=[
            pltpu.VMEM(innovations.shape, BF16),
            pltpu.SMEM((levels, 2), jnp.int32),
            pltpu.SMEM((levels, 2), jnp.int32),
            pltpu.VMEM((3, levels, ext, cols), F32),
            pltpu.VMEM((8, 2, HALO, cols), F32),
            pltpu.VMEM((2, HALO, cols), F32),
            pltpu.VMEM((levels, ext, cols), F32),
            pltpu.VMEM((8, HALO, cols), F32),
            pltpu.VMEM((3, HALO, cols), F32),
            pltpu.VMEM((levels, ext, cols), F32),
            pltpu.VMEM((group, 1, cols), F32),
            dma((6,)), dma((8,)), dma((8,)), dma((16,)), dma((16,)), dma((group,)), dma((group,)),
        ],
        compiler_params=pltpu.CompilerParams(
            collective_id=0, has_side_effects=True
        ),
    )(innovations, restrict_offsets, prolong_offsets, east, north, weight)


def solution(mesh):
    sizes = tuple(mesh.shape[axis] for axis in ("gx", "gy", "lev"))
    inner = P(("ens", "lev"), "gx", "gy")
    in_specs = (P("ens", "lev", "gx", "gy"), P("lev", None), P("lev", None), inner, inner, inner)
    return jax.shard_map(
        functools.partial(on_device, sizes), mesh=mesh, in_specs=in_specs,
        out_specs=(inner, inner), check_vma=False,
    )
```

```python
import functools

import jax
import jax.numpy as jnp
from jax import lax
from jax.experimental import pallas as pl
from jax.experimental.pallas import tpu as pltpu
from jax.sharding import PartitionSpec as P

MESH = pl.DeviceIdType.MESH
HALO = 8
SIDES = tuple((dx, dy) for dx in (1, -1, 0) for dy in (1, -1, 0) if dx or dy)
F32, BF16 = jnp.float32, jnp.bfloat16


def repeat(offsets, body):
    if len(offsets) <= 16:
        for k in offsets:
            body(k)
    else:
        lax.fori_loop(1, len(offsets) + 1, lambda k, carry: (body(k), carry)[1], 0)


def split(values):
    high = values.astype(BF16)
    return high, (values - high.astype(F32)).astype(BF16)


def dot(a, b):
    return jnp.dot(a, b, preferred_element_type=F32)


def split_dot(values, weights):
    high, low = split(values)
    return dot(high, weights) + dot(low, weights)


def iota(shape, dim):
    return lax.broadcasted_iota(jnp.int32, shape, dim)


def kernel(
    sizes, inn_hbm, r_hbm, p_hbm, east, north, weight, out, res, inn, r_off, p_off, coef, c_rim, c_pack, g_near, g_rim, g_pack, near_out,
    red, local, c_send, c_recv, g_send, g_recv, r_send, r_recv,
):
    nx, ny, nl = sizes
    group = nx * ny * nl
    steps, levels, fine_x, fine_y = inn.shape
    rows, cols = fine_x // 4, fine_y // 4
    ext = rows + 2 * HALO
    wide = 2 * cols
    ix, iy, il = lax.axis_index("gx"), lax.axis_index("gy"), lax.axis_index("lev")
    me = (ix * ny + iy) * nl + il

    offsets = sorted(
        range(1, group),
        key=lambda k: (k % nl, k // (ny * nl) not in (0, 1, nx - 1), k // (ny * nl) == 0, k),
    )

    def peer_index(k):
        return (
            lax.rem(ix + k // (ny * nl), nx), lax.rem(iy + k // nl % ny, ny), lax.rem(il + k % nl, nl)
        )

    def peer(k):
        x, y, l = peer_index(k)
        return {"gx": x, "gy": y, "lev": l}

    loads = [
        pltpu.make_async_copy(src, dst, local.at[k])
        for k, (src, dst) in enumerate(
            [(ref, coef.at[field, :, pl.ds(HALO, rows)]) for field, ref in enumerate((east, north, weight))]
            + [(r_hbm, r_off), (inn_hbm, inn), (p_hbm, p_off)]
        )
    ]
    for load in loads:
        load.start()
    edge = jnp.zeros((3, levels, HALO, cols), F32)
    coef[:, :, :HALO] = edge
    coef[:, :, HALO + rows :] = edge
    for ref in (c_rim, g_near, g_rim):
        ref[...] = jnp.zeros_like(ref)
    barrier = pltpu.get_barrier_semaphore()
    repeat(offsets, lambda k: pl.semaphore_signal(barrier, inc=1, device_id=peer(k), device_id_type=MESH))
    def wrapped(shape, dim):
        lane = iota(shape, dim)
        return jnp.where(lane < wide - wide // 4, lane, lane - wide)

    a_shape = (steps * ext, steps * fine_x)
    a_row, a_col = iota(a_shape, 0), iota(a_shape, 1)
    a_same = a_row // ext == a_col // fine_x
    a_base = 0.25 * (a_col % fine_x - 4 * (a_row % ext - HALO)).astype(F32)
    a_base = jnp.where(a_same, a_base, 1e6)
    c_shape = (fine_y, wide)
    c_base = 0.25 * (iota(c_shape, 0) - 4 * wrapped(c_shape, 1)).astype(F32)

    def tent(base, offset):
        return jnp.maximum(0.5 - jnp.abs(base - (offset.astype(F32) + 0.5) * 0.25), 0.0).astype(BF16)

    loads[3].wait()
    a_mats = [tent(a_base, r_off[level, 0]) for level in range(levels)]
    c_mats = [tent(c_base, r_off[level, 1]) for level in range(levels)]

    pl.semaphore_wait(barrier, group - 1)
    for load in loads[:3]:
        load.wait()

    def present(dx, dy):
        x, y = ix + dx, iy + dy
        return (x >= 0) & (x < nx) & (y >= 0) & (y < ny)

    def remote(src, dst, send, recv, dx, dy):
        return pltpu.make_async_remote_copy(
            src_ref=src, dst_ref=dst, send_sem=send, recv_sem=recv,
            device_id={"gx": ix + dx, "gy": iy + dy}, device_id_type=MESH,
        )

    half = ext // 2
    coef_rows = {1: (rows, 0), -1: (HALO, HALO + rows)}
    half_rows = {1: (half, 0), -1: (0, half)}

    def coef_copies(number, dx, dy):
        sems = c_send.at[number], c_recv.at[number]
        if dy:
            return [remote(c_pack, c_rim.at[number], *sems, dx, dy)]
        src, dst = coef_rows[dx]
        return [remote(coef.at[:, :, pl.ds(src, HALO)], coef.at[:, :, pl.ds(dst, HALO)], *sems, dx, dy)]

    def g_copies(number, dx, dy):
        slot = {1: 0, -1: 1, 0: 2}[dy]
        found = [remote(g_pack.at[slot], g_rim.at[number], g_send.at[number], g_recv.at[number], dx, dy)]
        if dy == 0:
            src, dst = half_rows[dx]
            extra = len(SIDES) + number
            found.append(remote(
                near_out.at[:, pl.ds(src, half)], g_near.at[:, pl.ds(dst, half)],
                g_send.at[extra], g_recv.at[extra], dx, dy,
            ))
        return found

    def start_all(make):
        for number, (dx, dy) in enumerate(SIDES):
            @pl.when(present(dx, dy))
            def _():
                for copy in make(number, dx, dy):
                    copy.start()

    def wait_recv_all(make):
        for number, (dx, dy) in enumerate(SIDES):
            @pl.when(present(-dx, -dy))
            def _():
                for copy in make(number, dx, dy):
                    copy.wait_recv()

    def wait_send_all(make):
        for number, (dx, dy) in enumerate(SIDES):
            @pl.when(present(dx, dy))
            def _():
                for copy in make(number, dx, dy):
                    copy.wait_send()

    tile_lane = iota((HALO, cols), 1)
    window = (tile_lane + HALO) // (2 * HALO) % (cols // (2 * HALO))
    upper = (tile_lane + HALO) % (2 * HALO) < HALO

    def turn(tile, windows):
        shift = windows * 2 * HALO % cols
        return pltpu.roll(tile, shift, 1) if shift else tile

    def pack(tiles):
        packed = jnp.zeros((HALO, cols), F32)
        for k, tile in enumerate(tiles):
            packed = jnp.where(window == k, turn(tile, k), packed)
        return packed

    def unpack(packed, k):
        return jnp.where(window == 0, turn(packed, -k), 0.0)

    row_tiles = rows // HALO

    def own_tiles(field):
        return [
            coef[field, level, HALO * (1 + r) : HALO * (2 + r), :]
            for level in range(levels) for r in range(row_tiles)
        ]

    c_pack[0] = pack(own_tiles(0) + own_tiles(1))
    c_pack[1] = pack(own_tiles(2))

    def arrived(dx, dy):
        return SIDES.index((-dx, -dy))

    start_all(coef_copies)

    loads[4].wait()
    restricted = []
    for level in range(levels):
        fine = inn[:, level].reshape(steps * fine_x, fine_y)
        part = dot(a_mats[level], fine)
        restricted.append(split_dot(part, c_mats[level]))

    def at_time(t):
        return jnp.concatenate([r[t * ext : (t + 1) * ext] for r in restricted], axis=0)

    wait_recv_all(coef_copies)
    rims = [
        jnp.where(upper, c_rim[arrived(dx, -1)], c_rim[arrived(dx, 1)]) for dx in (-1, 0, 1)
    ]

    def extended(field):
        part, first = field // 2, field % 2 * levels * row_tiles
        far_tiles = []
        for level in range(levels):
            k = first + level * row_tiles
            far_tiles.append(unpack(rims[0][part], k + row_tiles - 1))
            far_tiles += [unpack(rims[1][part], k + r) for r in range(row_tiles)]
            far_tiles.append(unpack(rims[2][part], k))
        near = coef[field].reshape(levels * ext, cols)
        return jnp.concatenate([near, jnp.concatenate(far_tiles, axis=0)], axis=1)

    e, n, w_obs = extended(0), extended(1), extended(2)
    stay = 1.0 - e - n
    total_rows = levels * ext

    def forward(x):
        return stay * x + e * pltpu.roll(x, 1, 0) + n * pltpu.roll(x, 1, 1)

    def adjoint(y):
        return stay * y + pltpu.roll(e * y, total_rows - 1, 0) + pltpu.roll(n * y, wide - 1, 1)

    lam = w_obs * at_time(steps - 1)
    for t in range(steps - 2, -1, -1):
        lam = adjoint(lam) + w_obs * at_time(t)
    mine = adjoint(lam)
    near, far = mine[:, :cols], mine[:, cols:]
    tiles = total_rows // HALO
    near_pack = pack([near[HALO * k : HALO * (k + 1)] for k in range(tiles)])
    far_pack = pack([far[HALO * k : HALO * (k + 1)] for k in range(tiles)])
    g_pack[0] = jnp.where(upper, near_pack, far_pack)
    g_pack[1] = jnp.where(upper, far_pack, near_pack)
    g_pack[2] = far_pack
    near_out[...] = near.reshape(levels, ext, cols)
    start_all(g_copies)

    m_shape = (total_rows, wide)
    m_row = iota(m_shape, 0) % ext - HALO + ix * rows
    m_col = wrapped(m_shape, 1) + iy * cols
    inside = (m_row >= 0) & (m_row < nx * rows) & (m_col >= 0) & (m_col < ny * cols)

    wait_recv_all(g_copies)
    ext_tiles = ext // HALO
    first_half = window % ext_tiles < ext_tiles // 2

    def shifted(dy):
        back = turn(g_rim[arrived(-1, dy)], -(ext_tiles // 2))
        ahead = turn(g_rim[arrived(1, dy)], ext_tiles // 2)
        return jnp.where(first_half, back, ahead)

    from_left = g_rim[arrived(0, -1)] + shifted(-1)
    from_right = g_rim[arrived(0, 1)] + shifted(1)
    near_rim = jnp.where(upper, from_right, from_left)
    far_rim = jnp.where(upper, from_left, from_right) + shifted(0)

    def unpack_all(packed):
        return jnp.concatenate([unpack(packed, k) for k in range(tiles)], axis=0)

    beside = g_near[...].reshape(total_rows, cols)
    g = mine + jnp.concatenate([beside + unpack_all(near_rim), unpack_all(far_rim)], axis=1)
    g = jnp.where(inside, g, 0.0)

    def sweep_ahead(p):
        states = []
        for _ in range(steps):
            p = forward(p)
            states.append(p)
        return states, [w_obs * state for state in states]

    def sweep_back(weighted):
        lam = weighted[-1]
        for t in range(steps - 2, -1, -1):
            lam = adjoint(lam) + weighted[t]
        return adjoint(lam)

    def own(x):
        return [x[l * ext + HALO : l * ext + HALO + rows, :cols] for l in range(levels)]

    w = jnp.where(inside, g + sweep_back(sweep_ahead(g)[1]), 0.0)
    states, weighted = sweep_ahead(w)
    g_own, w_own = own(g), own(w)
    norms = [
        sum((x * y for x, y in zip(xs, ys)), u * u)
        for u, xs, ys in zip(w_own, zip(*map(own, states)), zip(*map(own, weighted)))
    ]

    def partial(a, b):
        return sum(jnp.sum(x * y, axis=0, keepdims=True) for x, y in zip(a, b))

    gram = jnp.concatenate(
        [partial(g_own, g_own), partial(g_own, w_own), partial(w_own, w_own), partial(norms, [1.0] * levels)]
        + [jnp.zeros((4, cols), F32)], axis=0,
    )
    spread = jnp.sum(gram, axis=1, keepdims=True)
    quarter = iota((8, cols), 1) // (cols // 4)
    red[me] = jnp.sum(jnp.where(quarter == iota((8, cols), 0), spread, 0.0), axis=0, keepdims=True)

    def red_send(k):
        return pltpu.make_async_remote_copy(
            src_ref=red.at[me], dst_ref=red.at[me], send_sem=r_send, recv_sem=r_recv,
            device_id=peer(k), device_id_type=MESH,
        )

    others = pl.ds(0, group - 1)
    red_all = pltpu.make_async_remote_copy(
        src_ref=red.at[others], dst_ref=red.at[others], send_sem=r_send, recv_sem=r_recv,
        device_id=peer(1), device_id_type=MESH,
    )

    far_first = sorted(offsets, key=lambda k: (k // (ny * nl) in (0, 2), k // (ny * nl) == 0, -(k // nl % ny), k))
    repeat(far_first, lambda k: red_send(k).start())

    v_own = own(w + sweep_back(weighted))
    q_shape = (wide, fine_y)
    q_base = 0.25 * iota(q_shape, 1).astype(F32) - wrapped(q_shape, 0).astype(F32)
    b_shape = (fine_x, 2 * ext)
    b_base = 0.25 * iota(b_shape, 0).astype(F32) - (iota(b_shape, 1) % ext - HALO).astype(F32)

    def hat(base, offset):
        return jnp.maximum(1.0 - jnp.abs(base - offset.astype(F32) * 0.25), 0.0).astype(BF16)

    loads[5].wait()
    fine_parts = []
    for level in range(levels):
        both = jnp.concatenate([x[level * ext : (level + 1) * ext] for x in (g, w)], axis=0)
        across = split_dot(both, hat(q_base, p_off[level, 1]))
        up = hat(b_base, p_off[level, 0])
        fine_parts.append([
            dot(up, jnp.concatenate(split(across[k * ext : (k + 1) * ext]), axis=0)) for k in range(2)
        ])

    red_all.wait_recv()
    sums = jnp.sum(red[...], axis=0)
    gg, gw, ww, wv = (sums[:, k * (cols // 4)][:, None] for k in range(4))
    alpha = gg / gw
    rr = gg - 2.0 * alpha * gw + alpha * alpha * ww
    beta = rr / gg
    more = 1.0 + beta
    curvature = more * more * gw - 2.0 * alpha * more * ww + alpha * alpha * wv
    alpha_1 = rr / curvature
    from_g = alpha + alpha_1 * more
    from_w = -alpha_1 * alpha
    res_w = -(alpha + alpha_1 * more)
    res_v = alpha_1 * alpha
    for level in range(levels):
        out[level] = from_g * fine_parts[level][0] + from_w * fine_parts[level][1]
        res[level] = g_own[level] + res_w * w_own[level] + res_v * v_own[level]

    wait_send_all(coef_copies)
    wait_send_all(g_copies)
    red_all.wait_send()


def store(increment, residual, out, res, sems):
    copies = [
        pltpu.make_async_copy(src, dst, sems.at[k])
        for k, (src, dst) in enumerate([(increment, out), (residual, res)])
    ]
    for copy in copies:
        copy.start()
    for copy in copies:
        copy.wait()


def on_device(sizes, innovations, restrict_offsets, prolong_offsets, east, north, weight):
    _, levels, fine_x, fine_y = innovations.shape
    rows, cols = fine_x // 4, fine_y // 4
    ext = rows + 2 * HALO
    group = sizes[0] * sizes[1] * sizes[2]
    vmem = pl.BlockSpec(memory_space=pltpu.VMEM)
    hbm = pl.BlockSpec(memory_space=pltpu.HBM)
    dma = pltpu.SemaphoreType.DMA
    made = pl.pallas_call(
        functools.partial(kernel, sizes),
        out_shape=(
            pltpu.VMEM((levels, fine_x, fine_y), F32),
            pltpu.VMEM((levels, rows, cols), F32),
        ),
        in_specs=[hbm] * 6,
        out_specs=(vmem, vmem),
        scratch_shapes=[
            pltpu.VMEM(innovations.shape, BF16),
            pltpu.SMEM((levels, 2), jnp.int32),
            pltpu.SMEM((levels, 2), jnp.int32),
            pltpu.VMEM((3, levels, ext, cols), F32),
            pltpu.VMEM((8, 2, HALO, cols), F32),
            pltpu.VMEM((2, HALO, cols), F32),
            pltpu.VMEM((levels, ext, cols), F32),
            pltpu.VMEM((8, HALO, cols), F32),
            pltpu.VMEM((3, HALO, cols), F32),
            pltpu.VMEM((levels, ext, cols), F32),
            pltpu.VMEM((group, 1, cols), F32),
            dma((6,)), dma((8,)), dma((8,)), dma((16,)), dma((16,)), dma, dma,
        ],
        compiler_params=pltpu.CompilerParams(
            collective_id=0, has_side_effects=True
        ),
    )(innovations, restrict_offsets, prolong_offsets, east, north, weight)
    return pl.pallas_call(
        store,
        out_shape=tuple(jax.ShapeDtypeStruct(x.shape, F32) for x in made),
        in_specs=[vmem, vmem],
        out_specs=(hbm, hbm),
        scratch_shapes=[dma((2,))],
    )(*(pltpu.with_memory_space_constraint(x, pltpu.VMEM) for x in made))


def solution(mesh):
    sizes = tuple(mesh.shape[axis] for axis in ("gx", "gy", "lev"))
    inner = P(("ens", "lev"), "gx", "gy")
    in_specs = (P("ens", "lev", "gx", "gy"), P("lev", None), P("lev", None), inner, inner, inner)
    return jax.shard_map(
        functools.partial(on_device, sizes), mesh=mesh, in_specs=in_specs,
        out_specs=(inner, inner), check_vma=False,
    )
```

```python
import functools

import jax
import jax.numpy as jnp
from jax import lax
from jax.experimental import pallas as pl
from jax.experimental.pallas import tpu as pltpu
from jax.sharding import PartitionSpec as P

MESH = pl.DeviceIdType.MESH
HALO = 8
SIDES = tuple((dx, dy) for dx in (1, -1, 0) for dy in (1, -1, 0) if dx or dy)
F32, BF16 = jnp.float32, jnp.bfloat16


def repeat(offsets, body):
    if len(offsets) <= 16:
        for k in offsets:
            body(k)
    else:
        lax.fori_loop(1, len(offsets) + 1, lambda k, carry: (body(k), carry)[1], 0)


def split(values):
    high = values.astype(BF16)
    return high, (values - high.astype(F32)).astype(BF16)


def dot(a, b):
    return jnp.dot(a, b, preferred_element_type=F32)


def split_dot(values, weights):
    high, low = split(values)
    return dot(high, weights) + dot(low, weights)


def iota(shape, dim):
    return lax.broadcasted_iota(jnp.int32, shape, dim)


def kernel(
    sizes, inn_hbm, r_hbm, p_hbm, east, north, weight, out, res, inn, r_off, p_off, coef, c_rim, c_pack, g_near, g_rim, g_pack, near_out,
    red, local, c_send, c_recv, g_send, g_recv, r_send, r_recv,
):
    nx, ny, nl = sizes
    group = nx * ny * nl
    steps, levels, fine_x, fine_y = inn.shape
    rows, cols = fine_x // 4, fine_y // 4
    ext = rows + 2 * HALO
    wide = 2 * cols
    ix, iy, il = lax.axis_index("gx"), lax.axis_index("gy"), lax.axis_index("lev")
    me = (ix * ny + iy) * nl + il

    offsets = sorted(
        range(1, group),
        key=lambda k: (k % nl, k // (ny * nl) not in (0, 1, nx - 1), k // (ny * nl) == 0, k),
    )

    def peer_index(k):
        return (
            lax.rem(ix + k // (ny * nl), nx), lax.rem(iy + k // nl % ny, ny), lax.rem(il + k % nl, nl)
        )

    def peer(k):
        x, y, l = peer_index(k)
        return {"gx": x, "gy": y, "lev": l}

    loads = [
        pltpu.make_async_copy(src, dst, local.at[k])
        for k, (src, dst) in enumerate(
            [(ref, coef.at[field, :, pl.ds(HALO, rows)]) for field, ref in enumerate((east, north, weight))]
            + [(r_hbm, r_off), (inn_hbm, inn), (p_hbm, p_off)]
        )
    ]
    for load in loads:
        load.start()
    edge = jnp.zeros((3, levels, HALO, cols), F32)
    coef[:, :, :HALO] = edge
    coef[:, :, HALO + rows :] = edge
    for ref in (c_rim, g_near, g_rim):
        ref[...] = jnp.zeros_like(ref)
    def present(dx, dy):
        x, y = ix + dx, iy + dy
        return (x >= 0) & (x < nx) & (y >= 0) & (y < ny)

    barrier = pltpu.get_barrier_semaphore()
    if nx <= 4 and ny <= 2 and nl == 2:
        greeted = [(dx, dy, 0) for dx, dy in sorted(SIDES, key=lambda side: abs(side[0]) + abs(side[1]))]
        greeted += [(1, 0, 1), (-1, 0, 1)]
        count = 1
        for dx, dy, other in greeted:
            here = present(dx, dy)
            count += here.astype(jnp.int32)

            @pl.when(here)
            def _():
                target = {"gx": ix + dx, "gy": iy + dy, "lev": 1 - il if other else il}
                pl.semaphore_signal(barrier, inc=1, device_id=target, device_id_type=MESH)

        pl.semaphore_signal(barrier, inc=1, device_id={"lev": 1 - il}, device_id_type=MESH)
        pl.semaphore_wait(barrier, count)
    else:
        repeat(offsets, lambda k: pl.semaphore_signal(barrier, inc=1, device_id=peer(k), device_id_type=MESH))
        pl.semaphore_wait(barrier, group - 1)
    for load in loads[:3]:
        load.wait()

    def remote(src, dst, send, recv, dx, dy):
        return pltpu.make_async_remote_copy(
            src_ref=src, dst_ref=dst, send_sem=send, recv_sem=recv,
            device_id={"gx": ix + dx, "gy": iy + dy}, device_id_type=MESH,
        )

    half = ext // 2
    coef_rows = {1: (rows, 0), -1: (HALO, HALO + rows)}
    half_rows = {1: (half, 0), -1: (0, half)}

    def coef_copies(number, dx, dy):
        sems = c_send.at[number], c_recv.at[number]
        if dy:
            return [remote(c_pack, c_rim.at[number], *sems, dx, dy)]
        src, dst = coef_rows[dx]
        return [remote(coef.at[:, :, pl.ds(src, HALO)], coef.at[:, :, pl.ds(dst, HALO)], *sems, dx, dy)]

    def g_copies(number, dx, dy):
        slot = {1: 0, -1: 1, 0: 2}[dy]
        found = [remote(g_pack.at[slot], g_rim.at[number], g_send.at[number], g_recv.at[number], dx, dy)]
        if dy == 0:
            src, dst = half_rows[dx]
            extra = len(SIDES) + number
            found.append(remote(
                near_out.at[:, pl.ds(src, half)], g_near.at[:, pl.ds(dst, half)],
                g_send.at[extra], g_recv.at[extra], dx, dy,
            ))
        return found

    def start_all(make):
        for number, (dx, dy) in enumerate(SIDES):
            @pl.when(present(dx, dy))
            def _():
                for copy in make(number, dx, dy):
                    copy.start()

    def wait_recv_all(make):
        for number, (dx, dy) in enumerate(SIDES):
            @pl.when(present(-dx, -dy))
            def _():
                for copy in make(number, dx, dy):
                    copy.wait_recv()

    def wait_send_all(make):
        for number, (dx, dy) in enumerate(SIDES):
            @pl.when(present(dx, dy))
            def _():
                for copy in make(number, dx, dy):
                    copy.wait_send()

    tile_lane = iota((HALO, cols), 1)
    window = (tile_lane + HALO) // (2 * HALO) % (cols // (2 * HALO))
    upper = (tile_lane + HALO) % (2 * HALO) < HALO

    def turn(tile, windows):
        shift = windows * 2 * HALO % cols
        return pltpu.roll(tile, shift, 1) if shift else tile

    def pack(tiles):
        packed = jnp.zeros((HALO, cols), F32)
        for k, tile in enumerate(tiles):
            packed = jnp.where(window == k, turn(tile, k), packed)
        return packed

    def unpack(packed, k):
        return jnp.where(window == 0, turn(packed, -k), 0.0)

    row_tiles = rows // HALO

    def own_tiles(field):
        return [
            coef[field, level, HALO * (1 + r) : HALO * (2 + r), :]
            for level in range(levels) for r in range(row_tiles)
        ]

    c_pack[0] = pack(own_tiles(0) + own_tiles(1))
    c_pack[1] = pack(own_tiles(2))

    def arrived(dx, dy):
        return SIDES.index((-dx, -dy))

    start_all(coef_copies)

    def wrapped(shape, dim):
        lane = iota(shape, dim)
        return jnp.where(lane < wide - wide // 4, lane, lane - wide)

    a_shape = (steps * ext, steps * fine_x)
    a_row, a_col = iota(a_shape, 0), iota(a_shape, 1)
    a_same = a_row // ext == a_col // fine_x
    a_base = 0.25 * (a_col % fine_x - 4 * (a_row % ext - HALO)).astype(F32)
    a_base = jnp.where(a_same, a_base, 1e6)
    c_shape = (fine_y, wide)
    c_base = 0.25 * (iota(c_shape, 0) - 4 * wrapped(c_shape, 1)).astype(F32)

    def tent(base, offset):
        return jnp.maximum(0.5 - jnp.abs(base - (offset.astype(F32) + 0.5) * 0.25), 0.0).astype(BF16)

    loads[3].wait()
    a_mats = [tent(a_base, r_off[level, 0]) for level in range(levels)]
    c_mats = [tent(c_base, r_off[level, 1]) for level in range(levels)]


    loads[4].wait()
    restricted = []
    for level in range(levels):
        fine = inn[:, level].reshape(steps * fine_x, fine_y)
        part = dot(a_mats[level], fine)
        restricted.append(split_dot(part, c_mats[level]))

    def at_time(t):
        return jnp.concatenate([r[t * ext : (t + 1) * ext] for r in restricted], axis=0)

    wait_recv_all(coef_copies)
    rims = [
        jnp.where(upper, c_rim[arrived(dx, -1)], c_rim[arrived(dx, 1)]) for dx in (-1, 0, 1)
    ]

    def extended(field):
        part, first = field // 2, field % 2 * levels * row_tiles
        far_tiles = []
        for level in range(levels):
            k = first + level * row_tiles
            far_tiles.append(unpack(rims[0][part], k + row_tiles - 1))
            far_tiles += [unpack(rims[1][part], k + r) for r in range(row_tiles)]
            far_tiles.append(unpack(rims[2][part], k))
        near = coef[field].reshape(levels * ext, cols)
        return jnp.concatenate([near, jnp.concatenate(far_tiles, axis=0)], axis=1)

    e, n, w_obs = extended(0), extended(1), extended(2)
    stay = 1.0 - e - n
    total_rows = levels * ext

    def forward(x):
        return stay * x + e * pltpu.roll(x, 1, 0) + n * pltpu.roll(x, 1, 1)

    def adjoint(y):
        return stay * y + pltpu.roll(e * y, total_rows - 1, 0) + pltpu.roll(n * y, wide - 1, 1)

    lam = w_obs * at_time(steps - 1)
    for t in range(steps - 2, -1, -1):
        lam = adjoint(lam) + w_obs * at_time(t)
    mine = adjoint(lam)
    near, far = mine[:, :cols], mine[:, cols:]
    tiles = total_rows // HALO
    near_pack = pack([near[HALO * k : HALO * (k + 1)] for k in range(tiles)])
    far_pack = pack([far[HALO * k : HALO * (k + 1)] for k in range(tiles)])
    g_pack[0] = jnp.where(upper, near_pack, far_pack)
    g_pack[1] = jnp.where(upper, far_pack, near_pack)
    g_pack[2] = far_pack
    near_out[...] = near.reshape(levels, ext, cols)
    start_all(g_copies)

    m_shape = (total_rows, wide)
    m_row = iota(m_shape, 0) % ext - HALO + ix * rows
    m_col = wrapped(m_shape, 1) + iy * cols
    inside = (m_row >= 0) & (m_row < nx * rows) & (m_col >= 0) & (m_col < ny * cols)

    wait_recv_all(g_copies)
    ext_tiles = ext // HALO
    first_half = window % ext_tiles < ext_tiles // 2

    def shifted(dy):
        back = turn(g_rim[arrived(-1, dy)], -(ext_tiles // 2))
        ahead = turn(g_rim[arrived(1, dy)], ext_tiles // 2)
        return jnp.where(first_half, back, ahead)

    from_left = g_rim[arrived(0, -1)] + shifted(-1)
    from_right = g_rim[arrived(0, 1)] + shifted(1)
    near_rim = jnp.where(upper, from_right, from_left)
    far_rim = jnp.where(upper, from_left, from_right) + shifted(0)

    def unpack_all(packed):
        return jnp.concatenate([unpack(packed, k) for k in range(tiles)], axis=0)

    beside = g_near[...].reshape(total_rows, cols)
    g = mine + jnp.concatenate([beside + unpack_all(near_rim), unpack_all(far_rim)], axis=1)
    g = jnp.where(inside, g, 0.0)

    def sweep_ahead(p):
        states = []
        for _ in range(steps):
            p = forward(p)
            states.append(p)
        return states, [w_obs * state for state in states]

    def sweep_back(weighted):
        lam = weighted[-1]
        for t in range(steps - 2, -1, -1):
            lam = adjoint(lam) + weighted[t]
        return adjoint(lam)

    def own(x):
        return [x[l * ext + HALO : l * ext + HALO + rows, :cols] for l in range(levels)]

    w = jnp.where(inside, g + sweep_back(sweep_ahead(g)[1]), 0.0)
    states, weighted = sweep_ahead(w)
    g_own, w_own = own(g), own(w)
    norms = [
        sum((x * y for x, y in zip(xs, ys)), u * u)
        for u, xs, ys in zip(w_own, zip(*map(own, states)), zip(*map(own, weighted)))
    ]

    def partial(a, b):
        return sum(jnp.sum(x * y, axis=0, keepdims=True) for x, y in zip(a, b))

    gram = jnp.concatenate(
        [partial(g_own, g_own), partial(g_own, w_own), partial(w_own, w_own), partial(norms, [1.0] * levels)]
        + [jnp.zeros((4, cols), F32)], axis=0,
    )
    spread = jnp.sum(gram, axis=1, keepdims=True)
    quarter = iota((8, cols), 1) // (cols // 4)
    red[me] = jnp.sum(jnp.where(quarter == iota((8, cols), 0), spread, 0.0), axis=0, keepdims=True)

    def red_send(k):
        return pltpu.make_async_remote_copy(
            src_ref=red.at[me], dst_ref=red.at[me], send_sem=r_send, recv_sem=r_recv,
            device_id=peer(k), device_id_type=MESH,
        )

    others = pl.ds(0, group - 1)
    red_all = pltpu.make_async_remote_copy(
        src_ref=red.at[others], dst_ref=red.at[others], send_sem=r_send, recv_sem=r_recv,
        device_id=peer(1), device_id_type=MESH,
    )

    far_first = sorted(offsets, key=lambda k: (k // (ny * nl) in (0, 2), k // (ny * nl) == 0, -(k // nl % ny), k))
    repeat(far_first, lambda k: red_send(k).start())

    v_own = own(w + sweep_back(weighted))
    q_shape = (wide, fine_y)
    q_base = 0.25 * iota(q_shape, 1).astype(F32) - wrapped(q_shape, 0).astype(F32)
    b_shape = (fine_x, 2 * ext)
    b_base = 0.25 * iota(b_shape, 0).astype(F32) - (iota(b_shape, 1) % ext - HALO).astype(F32)

    def hat(base, offset):
        return jnp.maximum(1.0 - jnp.abs(base - offset.astype(F32) * 0.25), 0.0).astype(BF16)

    loads[5].wait()
    fine_parts = []
    for level in range(levels):
        both = jnp.concatenate([x[level * ext : (level + 1) * ext] for x in (g, w)], axis=0)
        across = split_dot(both, hat(q_base, p_off[level, 1]))
        up = hat(b_base, p_off[level, 0])
        fine_parts.append([
            dot(up, jnp.concatenate(split(across[k * ext : (k + 1) * ext]), axis=0)) for k in range(2)
        ])

    red_all.wait_recv()
    sums = jnp.sum(red[...], axis=0)
    gg, gw, ww, wv = (sums[:, k * (cols // 4)][:, None] for k in range(4))
    alpha = gg / gw
    rr = gg - 2.0 * alpha * gw + alpha * alpha * ww
    beta = rr / gg
    more = 1.0 + beta
    curvature = more * more * gw - 2.0 * alpha * more * ww + alpha * alpha * wv
    alpha_1 = rr / curvature
    from_g = alpha + alpha_1 * more
    from_w = -alpha_1 * alpha
    res_w = -(alpha + alpha_1 * more)
    res_v = alpha_1 * alpha
    for level in range(levels):
        out[level] = from_g * fine_parts[level][0] + from_w * fine_parts[level][1]
        res[level] = g_own[level] + res_w * w_own[level] + res_v * v_own[level]

    wait_send_all(coef_copies)
    wait_send_all(g_copies)
    red_all.wait_send()


def store(increment, residual, out, res, sems):
    copies = [
        pltpu.make_async_copy(src, dst, sems.at[k])
        for k, (src, dst) in enumerate([(increment, out), (residual, res)])
    ]
    for copy in copies:
        copy.start()
    for copy in copies:
        copy.wait()


def on_device(sizes, innovations, restrict_offsets, prolong_offsets, east, north, weight):
    _, levels, fine_x, fine_y = innovations.shape
    rows, cols = fine_x // 4, fine_y // 4
    ext = rows + 2 * HALO
    group = sizes[0] * sizes[1] * sizes[2]
    vmem = pl.BlockSpec(memory_space=pltpu.VMEM)
    hbm = pl.BlockSpec(memory_space=pltpu.HBM)
    dma = pltpu.SemaphoreType.DMA
    made = pl.pallas_call(
        functools.partial(kernel, sizes),
        out_shape=(
            pltpu.VMEM((levels, fine_x, fine_y), F32),
            pltpu.VMEM((levels, rows, cols), F32),
        ),
        in_specs=[hbm] * 6,
        out_specs=(vmem, vmem),
        scratch_shapes=[
            pltpu.VMEM(innovations.shape, BF16),
            pltpu.SMEM((levels, 2), jnp.int32),
            pltpu.SMEM((levels, 2), jnp.int32),
            pltpu.VMEM((3, levels, ext, cols), F32),
            pltpu.VMEM((8, 2, HALO, cols), F32),
            pltpu.VMEM((2, HALO, cols), F32),
            pltpu.VMEM((levels, ext, cols), F32),
            pltpu.VMEM((8, HALO, cols), F32),
            pltpu.VMEM((3, HALO, cols), F32),
            pltpu.VMEM((levels, ext, cols), F32),
            pltpu.VMEM((group, 1, cols), F32),
            dma((6,)), dma((8,)), dma((8,)), dma((16,)), dma((16,)), dma, dma,
        ],
        compiler_params=pltpu.CompilerParams(
            collective_id=0, has_side_effects=True
        ),
    )(innovations, restrict_offsets, prolong_offsets, east, north, weight)
    return pl.pallas_call(
        store,
        out_shape=tuple(jax.ShapeDtypeStruct(x.shape, F32) for x in made),
        in_specs=[vmem, vmem],
        out_specs=(hbm, hbm),
        scratch_shapes=[dma((2,))],
    )(*(pltpu.with_memory_space_constraint(x, pltpu.VMEM) for x in made))


def solution(mesh):
    sizes = tuple(mesh.shape[axis] for axis in ("gx", "gy", "lev"))
    inner = P(("ens", "lev"), "gx", "gy")
    in_specs = (P("ens", "lev", "gx", "gy"), P("lev", None), P("lev", None), inner, inner, inner)
    return jax.shard_map(
        functools.partial(on_device, sizes), mesh=mesh, in_specs=in_specs,
        out_specs=(inner, inner), check_vma=False,
    )
```

```python
import functools

import jax
import jax.numpy as jnp
from jax import lax
from jax.experimental import pallas as pl
from jax.experimental.pallas import tpu as pltpu
from jax.sharding import PartitionSpec as P

MESH = pl.DeviceIdType.MESH
HALO = 8
SIDES = tuple((dx, dy) for dx in (1, -1, 0) for dy in (1, -1, 0) if dx or dy)
F32, BF16 = jnp.float32, jnp.bfloat16


def repeat(offsets, body):
    if len(offsets) <= 16:
        for k in offsets:
            body(k)
    else:
        lax.fori_loop(1, len(offsets) + 1, lambda k, carry: (body(k), carry)[1], 0)


def split(values):
    high = values.astype(BF16)
    return high, (values - high.astype(F32)).astype(BF16)


def dot(a, b):
    return jnp.dot(a, b, preferred_element_type=F32)


def split_dot(values, weights):
    high, low = split(values)
    return dot(high, weights) + dot(low, weights)


def iota(shape, dim):
    return lax.broadcasted_iota(jnp.int32, shape, dim)


def kernel(
    sizes, inn_hbm, r_hbm, p_hbm, east, north, weight, out, res, inn, r_off, p_off, coef, c_rim, c_pack, g_near, g_rim, g_pack, near_out,
    red, local, c_send, c_recv, g_send, g_recv, r_send, r_recv,
):
    nx, ny, nl = sizes
    group = nx * ny * nl
    steps, levels, fine_x, fine_y = inn.shape
    rows, cols = fine_x // 4, fine_y // 4
    ext = rows + 2 * HALO
    wide = 2 * cols
    ix, iy, il = lax.axis_index("gx"), lax.axis_index("gy"), lax.axis_index("lev")
    me = (ix * ny + iy) * nl + il

    offsets = sorted(
        range(1, group),
        key=lambda k: (k % nl, k // (ny * nl) not in (0, 1, nx - 1), k // (ny * nl) == 0, k),
    )

    def peer_index(k):
        return (
            lax.rem(ix + k // (ny * nl), nx), lax.rem(iy + k // nl % ny, ny), lax.rem(il + k % nl, nl)
        )

    def peer(k):
        x, y, l = peer_index(k)
        return {"gx": x, "gy": y, "lev": l}

    loads = [
        pltpu.make_async_copy(src, dst, local.at[k])
        for k, (src, dst) in enumerate(
            [(ref, coef.at[field, :, pl.ds(HALO, rows)]) for field, ref in enumerate((east, north, weight))]
            + [(r_hbm, r_off), (inn_hbm, inn), (p_hbm, p_off)]
        )
    ]
    for load in loads:
        load.start()
    edge = jnp.zeros((3, levels, HALO, cols), F32)
    coef[:, :, :HALO] = edge
    coef[:, :, HALO + rows :] = edge
    for ref in (c_rim, g_near, g_rim):
        ref[...] = jnp.zeros_like(ref)
    def present(dx, dy):
        x, y = ix + dx, iy + dy
        return (x >= 0) & (x < nx) & (y >= 0) & (y < ny)

    barrier = pltpu.get_barrier_semaphore()
    if nx <= 4 and ny <= 2 and nl == 2:
        greeted = [(dx, dy, 0) for dx, dy in sorted(SIDES, key=lambda side: abs(side[0]) + abs(side[1]))]
        greeted += [(1, 0, 1), (-1, 0, 1)]
        count = 1
        for dx, dy, other in greeted:
            here = present(dx, dy)
            count += here.astype(jnp.int32)

            @pl.when(here)
            def _():
                target = {"gx": ix + dx, "gy": iy + dy, "lev": 1 - il if other else il}
                pl.semaphore_signal(barrier, inc=1, device_id=target, device_id_type=MESH)

        pl.semaphore_signal(barrier, inc=1, device_id={"lev": 1 - il}, device_id_type=MESH)
        pl.semaphore_wait(barrier, count)
    else:
        repeat(offsets, lambda k: pl.semaphore_signal(barrier, inc=1, device_id=peer(k), device_id_type=MESH))
        pl.semaphore_wait(barrier, group - 1)
    for load in loads[:3]:
        load.wait()

    def remote(src, dst, send, recv, dx, dy):
        return pltpu.make_async_remote_copy(
            src_ref=src, dst_ref=dst, send_sem=send, recv_sem=recv,
            device_id={"gx": ix + dx, "gy": iy + dy}, device_id_type=MESH,
        )

    half = ext // 2
    coef_rows = {1: (rows, 0), -1: (HALO, HALO + rows)}
    half_end = levels * half

    def coef_copies(number, dx, dy):
        sems = c_send.at[number], c_recv.at[number]
        if dy:
            return [remote(c_pack, c_rim.at[number], *sems, dx, dy)]
        src, dst = coef_rows[dx]
        return [remote(coef.at[:, :, pl.ds(src, HALO)], coef.at[:, :, pl.ds(dst, HALO)], *sems, dx, dy)]

    def g_copies(number, dx, dy):
        sems = g_send.at[number], g_recv.at[number]
        if dy:
            return [remote(g_pack.at[0 if dy == 1 else 1], g_rim.at[number], *sems, dx, dy)]
        src, dst = (1, 0) if dx == 1 else (0, 1)
        return [remote(near_out.at[src], g_near.at[dst], *sems, dx, dy)]

    def start_all(make):
        for number, (dx, dy) in enumerate(SIDES):
            @pl.when(present(dx, dy))
            def _():
                for copy in make(number, dx, dy):
                    copy.start()

    def wait_recv_all(make):
        for number, (dx, dy) in enumerate(SIDES):
            @pl.when(present(-dx, -dy))
            def _():
                for copy in make(number, dx, dy):
                    copy.wait_recv()

    def wait_send_all(make):
        for number, (dx, dy) in enumerate(SIDES):
            @pl.when(present(dx, dy))
            def _():
                for copy in make(number, dx, dy):
                    copy.wait_send()

    tile_lane = iota((HALO, cols), 1)
    window = (tile_lane + HALO) // (2 * HALO) % (cols // (2 * HALO))
    upper = (tile_lane + HALO) % (2 * HALO) < HALO

    def turn(tile, windows):
        shift = windows * 2 * HALO % cols
        return pltpu.roll(tile, shift, 1) if shift else tile

    def pack(tiles):
        packed = jnp.zeros((HALO, cols), F32)
        for k, tile in enumerate(tiles):
            packed = jnp.where(window == k, turn(tile, k), packed)
        return packed

    def unpack(packed, k):
        return jnp.where(window == 0, turn(packed, -k), 0.0)

    row_tiles = rows // HALO

    def own_tiles(field):
        return [
            coef[field, level, HALO * (1 + r) : HALO * (2 + r), :]
            for level in range(levels) for r in range(row_tiles)
        ]

    c_pack[0] = pack(own_tiles(0) + own_tiles(1))
    c_pack[1] = pack(own_tiles(2))

    def arrived(dx, dy):
        return SIDES.index((-dx, -dy))

    start_all(coef_copies)

    def wrapped(shape, dim):
        lane = iota(shape, dim)
        return jnp.where(lane < wide - wide // 4, lane, lane - wide)

    a_shape = (steps * ext, steps * fine_x)
    a_row, a_col = iota(a_shape, 0), iota(a_shape, 1)
    a_same = a_row // ext == a_col // fine_x
    a_base = 0.25 * (a_col % fine_x - 4 * (a_row % ext - HALO)).astype(F32)
    a_base = jnp.where(a_same, a_base, 1e6)
    c_shape = (fine_y, wide)
    c_base = 0.25 * (iota(c_shape, 0) - 4 * wrapped(c_shape, 1)).astype(F32)

    def tent(base, offset):
        return jnp.maximum(0.5 - jnp.abs(base - (offset.astype(F32) + 0.5) * 0.25), 0.0).astype(BF16)

    loads[3].wait()
    a_mats = [tent(a_base, r_off[level, 0]) for level in range(levels)]
    c_mats = [tent(c_base, r_off[level, 1]) for level in range(levels)]


    loads[4].wait()
    restricted = []
    for level in range(levels):
        fine = inn[:, level].reshape(steps * fine_x, fine_y)
        part = dot(a_mats[level], fine)
        restricted.append(split_dot(part, c_mats[level]))

    def at_time(t):
        return jnp.concatenate([r[t * ext : (t + 1) * ext] for r in restricted], axis=0)

    wait_recv_all(coef_copies)
    rims = [
        jnp.where(upper, c_rim[arrived(dx, -1)], c_rim[arrived(dx, 1)]) for dx in (-1, 0, 1)
    ]

    def extended(field):
        part, first = field // 2, field % 2 * levels * row_tiles
        far_tiles = []
        for level in range(levels):
            k = first + level * row_tiles
            far_tiles.append(unpack(rims[0][part], k + row_tiles - 1))
            far_tiles += [unpack(rims[1][part], k + r) for r in range(row_tiles)]
            far_tiles.append(unpack(rims[2][part], k))
        near = coef[field].reshape(levels * ext, cols)
        return jnp.concatenate([near, jnp.concatenate(far_tiles, axis=0)], axis=1)

    e, n, w_obs = extended(0), extended(1), extended(2)
    stay = 1.0 - e - n
    total_rows = levels * ext

    def forward(x):
        return stay * x + e * pltpu.roll(x, 1, 0) + n * pltpu.roll(x, 1, 1)

    def adjoint(y, added=None):
        here = stay * y if added is None else stay * y + added
        return here + pltpu.roll(e * y, total_rows - 1, 0) + pltpu.roll(n * y, wide - 1, 1)

    lam = w_obs * at_time(steps - 1)
    for t in range(steps - 2, -1, -1):
        lam = adjoint(lam, w_obs * at_time(t))
    mine = adjoint(lam)
    near, far = mine[:, :cols], mine[:, cols:]
    tiles = total_rows // HALO
    near_pack = pack([near[HALO * k : HALO * (k + 1)] for k in range(tiles)])
    far_pack = pack([far[HALO * k : HALO * (k + 1)] for k in range(tiles)])
    g_pack[0] = jnp.where(upper, near_pack, far_pack)
    g_pack[1] = jnp.where(upper, far_pack, near_pack)
    for side in range(2):
        for level in range(levels):
            start = level * ext + side * half
            near_out[side, level * half : (level + 1) * half] = near[start : start + half]
        near_out[side, half_end:] = far_pack
    start_all(g_copies)

    m_shape = (total_rows, wide)
    m_row = iota(m_shape, 0) % ext - HALO + ix * rows
    m_col = wrapped(m_shape, 1) + iy * cols
    inside = (m_row >= 0) & (m_row < nx * rows) & (m_col >= 0) & (m_col < ny * cols)

    wait_recv_all(g_copies)
    ext_tiles = ext // HALO
    first_half = window % ext_tiles < ext_tiles // 2

    def shifted(dy):
        if dy:
            back, ahead = g_rim[arrived(-1, dy)], g_rim[arrived(1, dy)]
        else:
            back, ahead = g_near[0, half_end:], g_near[1, half_end:]
        back, ahead = turn(back, -(ext_tiles // 2)), turn(ahead, ext_tiles // 2)
        return jnp.where(first_half, back, ahead)

    from_left = g_rim[arrived(0, -1)] + shifted(-1)
    from_right = g_rim[arrived(0, 1)] + shifted(1)
    near_rim = jnp.where(upper, from_right, from_left)
    far_rim = jnp.where(upper, from_left, from_right) + shifted(0)

    def unpack_all(packed):
        return jnp.concatenate([unpack(packed, k) for k in range(tiles)], axis=0)

    beside = jnp.concatenate([
        g_near[side, level * half : (level + 1) * half]
        for level in range(levels) for side in range(2)
    ], axis=0)
    g = mine + jnp.concatenate([beside + unpack_all(near_rim), unpack_all(far_rim)], axis=1)
    g = jnp.where(inside, g, 0.0)

    def sweep_ahead(p):
        states = []
        for _ in range(steps):
            p = forward(p)
            states.append(p)
        return states, [w_obs * state for state in states]

    def sweep_back(weighted, added):
        lam = weighted[-1]
        for t in range(steps - 2, -1, -1):
            lam = adjoint(lam, weighted[t])
        return adjoint(lam, added)

    def own(x):
        return [x[l * ext + HALO : l * ext + HALO + rows, :cols] for l in range(levels)]

    w = jnp.where(inside, sweep_back(sweep_ahead(g)[1], g), 0.0)
    states, weighted = sweep_ahead(w)
    g_own, w_own = own(g), own(w)
    norms = [
        sum((x * y for x, y in zip(xs, ys)), u * u)
        for u, xs, ys in zip(w_own, zip(*map(own, states)), zip(*map(own, weighted)))
    ]

    def partial(a, b):
        return sum(jnp.sum(x * y, axis=0, keepdims=True) for x, y in zip(a, b))

    gram = jnp.concatenate(
        [partial(g_own, g_own), partial(g_own, w_own), partial(w_own, w_own), partial(norms, [1.0] * levels)]
        + [jnp.zeros((4, cols), F32)], axis=0,
    )
    spread = jnp.sum(gram, axis=1, keepdims=True)
    quarter = iota((8, cols), 1) // (cols // 4)
    red[me] = jnp.sum(jnp.where(quarter == iota((8, cols), 0), spread, 0.0), axis=0, keepdims=True)

    def red_send(k):
        return pltpu.make_async_remote_copy(
            src_ref=red.at[me], dst_ref=red.at[me], send_sem=r_send, recv_sem=r_recv,
            device_id=peer(k), device_id_type=MESH,
        )

    others = pl.ds(0, group - 1)
    red_all = pltpu.make_async_remote_copy(
        src_ref=red.at[others], dst_ref=red.at[others], send_sem=r_send, recv_sem=r_recv,
        device_id=peer(1), device_id_type=MESH,
    )

    far_first = sorted(offsets, key=lambda k: (k // (ny * nl) in (0, 2), k // (ny * nl) == 0, -(k // nl % ny), k))
    repeat(far_first, lambda k: red_send(k).start())

    v_own = own(sweep_back(weighted, w))
    q_shape = (wide, fine_y)
    q_base = 0.25 * iota(q_shape, 1).astype(F32) - wrapped(q_shape, 0).astype(F32)
    b_shape = (fine_x, 2 * ext)
    b_base = 0.25 * iota(b_shape, 0).astype(F32) - (iota(b_shape, 1) % ext - HALO).astype(F32)

    def hat(base, offset):
        return jnp.maximum(1.0 - jnp.abs(base - offset.astype(F32) * 0.25), 0.0).astype(BF16)

    loads[5].wait()
    fine_parts = []
    for level in range(levels):
        both = jnp.concatenate([x[level * ext : (level + 1) * ext] for x in (g, w)], axis=0)
        across = split_dot(both, hat(q_base, p_off[level, 1]))
        up = hat(b_base, p_off[level, 0])
        fine_parts.append([
            dot(up, jnp.concatenate(split(across[k * ext : (k + 1) * ext]), axis=0)) for k in range(2)
        ])

    red_all.wait_recv()
    sums = jnp.sum(red[...], axis=0)
    gg, gw, ww, wv = (sums[:, k * (cols // 4)][:, None] for k in range(4))
    alpha = gg / gw
    rr = gg - 2.0 * alpha * gw + alpha * alpha * ww
    beta = rr / gg
    more = 1.0 + beta
    curvature = more * more * gw - 2.0 * alpha * more * ww + alpha * alpha * wv
    alpha_1 = rr / curvature
    from_g = alpha + alpha_1 * more
    from_w = -alpha_1 * alpha
    res_w = -(alpha + alpha_1 * more)
    res_v = alpha_1 * alpha
    for level in range(levels):
        out[level] = from_g * fine_parts[level][0] + from_w * fine_parts[level][1]
        res[level] = g_own[level] + res_w * w_own[level] + res_v * v_own[level]

    wait_send_all(coef_copies)
    wait_send_all(g_copies)
    red_all.wait_send()


def store(increment, residual, out, res, sems):
    copies = [
        pltpu.make_async_copy(src, dst, sems.at[k])
        for k, (src, dst) in enumerate([(increment, out), (residual, res)])
    ]
    for copy in copies:
        copy.start()
    for copy in copies:
        copy.wait()


def on_device(sizes, innovations, restrict_offsets, prolong_offsets, east, north, weight):
    _, levels, fine_x, fine_y = innovations.shape
    rows, cols = fine_x // 4, fine_y // 4
    ext = rows + 2 * HALO
    group = sizes[0] * sizes[1] * sizes[2]
    vmem = pl.BlockSpec(memory_space=pltpu.VMEM)
    hbm = pl.BlockSpec(memory_space=pltpu.HBM)
    dma = pltpu.SemaphoreType.DMA
    made = pl.pallas_call(
        functools.partial(kernel, sizes),
        out_shape=(
            pltpu.VMEM((levels, fine_x, fine_y), F32),
            pltpu.VMEM((levels, rows, cols), F32),
        ),
        in_specs=[hbm] * 6,
        out_specs=(vmem, vmem),
        scratch_shapes=[
            pltpu.VMEM(innovations.shape, BF16),
            pltpu.SMEM((levels, 2), jnp.int32),
            pltpu.SMEM((levels, 2), jnp.int32),
            pltpu.VMEM((3, levels, ext, cols), F32),
            pltpu.VMEM((8, 2, HALO, cols), F32),
            pltpu.VMEM((2, HALO, cols), F32),
            pltpu.VMEM((2, levels * ext // 2 + HALO, cols), F32),
            pltpu.VMEM((8, HALO, cols), F32),
            pltpu.VMEM((2, HALO, cols), F32),
            pltpu.VMEM((2, levels * ext // 2 + HALO, cols), F32),
            pltpu.VMEM((group, 1, cols), F32),
            dma((6,)), dma((8,)), dma((8,)), dma((8,)), dma((8,)), dma, dma,
        ],
        compiler_params=pltpu.CompilerParams(
            collective_id=0, has_side_effects=True
        ),
    )(innovations, restrict_offsets, prolong_offsets, east, north, weight)
    return pl.pallas_call(
        store,
        out_shape=tuple(jax.ShapeDtypeStruct(x.shape, F32) for x in made),
        in_specs=[vmem, vmem],
        out_specs=(hbm, hbm),
        scratch_shapes=[dma((2,))],
    )(*(pltpu.with_memory_space_constraint(x, pltpu.VMEM) for x in made))


def solution(mesh):
    sizes = tuple(mesh.shape[axis] for axis in ("gx", "gy", "lev"))
    inner = P(("ens", "lev"), "gx", "gy")
    in_specs = (P("ens", "lev", "gx", "gy"), P("lev", None), P("lev", None), inner, inner, inner)
    return jax.shard_map(
        functools.partial(on_device, sizes), mesh=mesh, in_specs=in_specs,
        out_specs=(inner, inner), check_vma=False,
    )
```
